128 devices in a mesh: gx: 8 (over z_lo, x), gy: 16 (over z_hi, y, core).
Axes of the slice: x: 4, y: 4, z: 4 (z_hi: 2, z_lo: 2; z = z_hi * 2 + z_lo), core: 2. Of those that a mesh axis runs over, the one named last changes fastest.
Arguments:
- samples: bfloat16 [1024, 262144], P(('gx', 'gy')), may hold values from -6 to 6
- interp: bfloat16 [2, 2048, 32, 128], P(None, ('gx', 'gy')), may hold values from -0.5 to 0.5
- translation: bfloat16 [7, 2, 2048, 32, 64], P(None, None, ('gx', 'gy')), may hold values from -0.5 to 0.5
- evaluate: bfloat16 [2, 262144, 32], P(None, ('gx', 'gy')), may hold values from -0.75 to 0.75
Outputs:
- radon: float32 [1024, 262144], P(None, ('gx', 'gy'))
The draws below stay inside these ranges and needn't reach their ends.
All inputs are finite; a program needn't handle non-finite values.
Results may differ from the reference program's by a relative error of at most 0.013.
Values may be sent and summed in bfloat16 or wider, within the bound.
A program may use at most 128 MiB of HBM per device.

```python
import jax
import jax.numpy as jnp
from jax import lax

RANK = 32
BOXES = 16
SRC_DEV = 2048
TGT_DEV = 2048
LEVELS = 7
SRC_BOX = 128
ALL_BOXES = 2048
RECORDS = 1024
SOURCES = 262144
TARGETS = 262144
DEVICES = 128


def block_levels(rng, dims, split, low, high):
    loudness = 1.0
    for dim, shards_of in split:
        draws = jax.random.uniform(jax.random.fold_in(jax.random.fold_in(rng, 6), dim), (shards_of,), jnp.float32, low / len(split), high / len(split))
        loudness = loudness * jnp.repeat(jnp.exp(draws), dims[dim] // shards_of).reshape((-1,) + (1,) * (len(dims) - 1 - dim))
    return loudness


def centred(own_key, dims, width, limit, pieces=(), kind=jnp.bfloat16):
    factor_of = block_levels(own_key, dims, pieces, -0.22, 0.18) if pieces else 1.0
    values = jax.random.normal(own_key, dims, jnp.float32) * width * factor_of
    return jnp.minimum(jnp.maximum(values, -limit), limit).astype(kind)


def setup_inputs(seed: int = 0) -> dict:
    keys = jax.random.split(jax.random.key(seed), 5)
    return {
        "samples": centred(keys[0], (RECORDS, SOURCES), 1.0, 6.0, ((0, 128),)),
        "interp": centred(keys[1], (2, ALL_BOXES, RANK, SRC_BOX), SRC_BOX ** -0.5, 0.5, ((1, 128),)),
        "translation": centred(keys[2], (LEVELS, 2, ALL_BOXES, RANK, 2 * RANK), (4 * RANK) ** -0.5, 0.5, ((2, 128),)),
        "evaluate": centred(keys[3], (2, TARGETS, RANK), (2 * RANK) ** -0.5, 0.75, ((1, 128),)),
    }


def box_product(weight, values):
    return jnp.einsum("gkj,gjr->gkr", weight, values)


def reference(samples, interp, translation, evaluate):
    blocks = DEVICES
    all_boxes = DEVICES * BOXES
    per_src = SRC_DEV // BOXES
    per_tgt = TGT_DEV // BOXES
    by_block = samples.reshape(RECORDS, blocks, BOXES, per_src).transpose(1, 0, 2, 3)
    spread = interp.reshape(2, blocks, BOXES, RANK, per_src).transpose(1, 0, 2, 3, 4)

    def start_block(pair):
        block_samples, block_spread = pair
        return jnp.einsum("cbks,rbs->cbkr", block_spread.astype(jnp.float32), block_samples.astype(jnp.float32)).astype(jnp.bfloat16)

    state = lax.map(start_block, (by_block, spread))
    state = state.transpose(1, 0, 2, 3, 4).reshape(2, all_boxes, RANK, RECORDS)
    for level in range(LEVELS):
        stride = 2 ** level
        current = state.astype(jnp.float32)
        grouped = current.reshape(2, blocks // (2 * stride), 2, stride, BOXES, RANK, RECORDS)
        partner = grouped[:, :, ::-1].reshape(2, all_boxes, RANK, RECORDS)
        weight = translation[level].astype(jnp.float32)
        own_w = weight[..., :RANK]
        far_w = weight[..., RANK:]
        real = (box_product(own_w[0], current[0]) - box_product(own_w[1], current[1])
                + box_product(far_w[0], partner[0]) - box_product(far_w[1], partner[1]))
        imag = (box_product(own_w[0], current[1]) + box_product(own_w[1], current[0])
                + box_product(far_w[0], partner[1]) + box_product(far_w[1], partner[0]))
        state = jnp.stack([real, imag]).astype(jnp.bfloat16)
    final = state.reshape(2, blocks, BOXES, RANK, RECORDS).transpose(1, 0, 2, 3, 4)
    table = evaluate.reshape(2, blocks, BOXES, per_tgt, RANK).transpose(1, 0, 2, 3, 4)

    def finish_block(pair):
        block_table, block_state = pair
        tab = block_table.astype(jnp.float32)
        sta = block_state.astype(jnp.float32)
        out = jnp.einsum("btk,bkr->rbt", tab[0], sta[0]) - jnp.einsum("btk,bkr->rbt", tab[1], sta[1])
        return out.reshape(RECORDS, BOXES * per_tgt)

    result = lax.map(finish_block, (table, final))
    return result.transpose(1, 0, 2).reshape(RECORDS, blocks * TGT_DEV)
```

```python
import jax
import jax.numpy as jnp
from jax import lax
from jax.experimental import pallas as pl
from jax.experimental.pallas import tpu as pltpu
from jax.sharding import PartitionSpec as P

MESH = pl.DeviceIdType.MESH
F32, BF16 = jnp.float32, jnp.bfloat16
ANY = pl.BlockSpec(memory_space=pl.ANY)
LIMIT = 56 * 2**20


def place():
    return lax.axis_index("gx"), lax.axis_index("gy")


def greet(devices):
    barrier = pltpu.get_barrier_semaphore()
    for device in devices:
        pl.semaphore_signal(barrier, inc=1, device_id=device, device_id_type=MESH)
    pl.semaphore_wait(barrier, len(devices))


def spread_kernel(samples, own_w, own_v, x, w, v, send, recv, here):
    gx, gy = place()
    y = (gy >> 1) & 3
    up = (gy & 9) | (((y + 1) & 3) << 1)
    down = (gy & 9) | (((y + 3) & 3) << 1)
    far = gy ^ 8
    core = gy ^ 1
    greet([(gx, up), (gx, down), (gx, far), (gx, core)] + [(gx ^ m, gy) for m in range(1, 8)])
    used = [0]

    def push(src, dst, device):
        k = used[0]
        used[0] = k + 1
        copy = pltpu.make_async_remote_copy(
            src_ref=src, dst_ref=dst, send_sem=send.at[k], recv_sem=recv.at[k],
            device_id=device, device_id_type=MESH)
        copy.start()
        return copy

    keep = [pltpu.make_async_copy(samples.at[gx], x.at[gx], here.at[0]),
            pltpu.make_async_copy(own_w, w.at[gy], here.at[1]),
            pltpu.make_async_copy(own_v, v.at[gx], here.at[2])]
    to_far = push(own_w, w.at[gy], (gx, far))
    to_up = push(own_w, w.at[gy], (gx, up))
    to_down = push(own_w, w.at[gy], (gx, down))
    sent = [push(samples.at[gx ^ m], x.at[gx], (gx ^ m, gy)) for m in range(1, 8)]
    to_core = [push(own_w, w.at[gy], (gx, core))]
    for copy in keep:
        copy.start()
    lo, hi = pl.ds(0, 8), pl.ds(8, 8)

    def relay(from_down, from_up, flip):
        a, b = down ^ flip, up ^ flip
        from_down.wait_recv()
        one = push(w.at[a, lo], w.at[a, lo], (gx, up))
        core_a = push(w.at[a], w.at[a], (gx, core))
        from_up.wait_recv()
        two = push(w.at[b, hi], w.at[b, hi], (gx, down))
        core_b = push(w.at[b], w.at[b], (gx, core))
        return [one, two], [core_a, core_b]

    halves, cores = relay(to_up, to_down, 0)
    to_core += cores
    to_far.wait_recv()
    far_up = push(w.at[far], w.at[far], (gx, up))
    far_down = push(w.at[far], w.at[far], (gx, down))
    to_core.append(push(w.at[far], w.at[far], (gx, core)))
    own_4 = push(own_v, v.at[gx], (gx ^ 4, gy))
    own_x = [push(own_v, v.at[gx], (gx ^ m, gy)) for m in (1, 2, 3)]
    far_halves, cores = relay(far_up, far_down, 8)
    to_core += cores
    own_4.wait_recv()
    mate = gx ^ 4
    next_x = [push(v.at[mate], v.at[mate], (gx ^ m, gy)) for m in (1, 2, 3)]
    for flip, pair in ((0, halves), (8, far_halves)):
        for copy in pair:
            copy.wait_recv()
        opposite = gy ^ 4 ^ flip
        to_core.append(push(w.at[opposite], w.at[opposite], (gx, core)))
    for copy in sent + to_core + own_x + next_x:
        copy.wait()
    for copy in [to_far, to_up, to_down, far_up, far_down, own_4] + halves + far_halves:
        copy.wait_send()
    for copy in keep:
        copy.wait()


def spread(samples, own_w, own_v):
    return pl.pallas_call(
        spread_kernel,
        out_shape=[jax.ShapeDtypeStruct(samples.shape, BF16),
                   jax.ShapeDtypeStruct((16,) + own_w.shape, BF16),
                   jax.ShapeDtypeStruct((8,) + own_v.shape, BF16)],
        in_specs=[ANY] * 3,
        out_specs=[ANY] * 3,
        scratch_shapes=[pltpu.SemaphoreType.DMA((40,)), pltpu.SemaphoreType.DMA((40,)),
                        pltpu.SemaphoreType.DMA((3,))],
        compiler_params=pltpu.CompilerParams(collective_id=1, has_side_effects=True),
        name="spread",
    )(samples, own_w, own_v)


def turn(pair, first):
    moved = pltpu.roll(pair, 64, 1)
    return jnp.where(first, -moved, moved).astype(BF16)


def low_kernel(x_ref, w_ref, o_ref, state, turned):
    first = lax.broadcasted_iota(jnp.int32, (32, 128), 1) < 64
    for g in range(16):
        rows = x_ref[:, g, 0].reshape(64, 128)
        table = w_ref[g, 0, 0:2].reshape(64, 128)
        got = lax.dot_general(table, rows, (((1,), (1,)), ((), ())), preferred_element_type=F32)
        pair = jnp.concatenate([got[:32], got[32:]], axis=1)
        state[0, g] = pair.astype(BF16)
        turned[0, g] = turn(pair, first)
    for level in range(4):
        now, later = level % 2, (level + 1) % 2
        for g in range(16):
            h = g ^ (1 << level)
            right = jnp.concatenate(
                [state[now, g], state[now, h], turned[now, g], turned[now, h]], axis=0)
            got = jnp.dot(w_ref[g, 0, 2 + level], right, preferred_element_type=F32)
            if level == 3:
                o_ref[g, 0] = got.astype(BF16)
            else:
                state[later, g] = got.astype(BF16)
                turned[later, g] = turn(got, first)


def low(x, w):
    return pl.pallas_call(
        low_kernel,
        grid=(16,),
        out_shape=jax.ShapeDtypeStruct((16, 16, 32, 128), BF16),
        in_specs=[pl.BlockSpec((8, 16, 1, 8, 128), lambda b: (0, 0, b, 0, 0)),
                  pl.BlockSpec((16, 1, 6, 32, 128), lambda b: (0, b, 0, 0, 0))],
        out_specs=pl.BlockSpec((16, 1, 32, 128), lambda b: (0, (b % 8) * 2 + b // 8, 0, 0)),
        scratch_shapes=[pltpu.VMEM((2, 16, 32, 128), BF16), pltpu.VMEM((2, 16, 32, 128), BF16)],
        compiler_params=pltpu.CompilerParams(vmem_limit_bytes=LIMIT),
        name="low",
    )(x, w)


def swap_kernel(o, t, send, recv, here):
    gx, gy = place()
    half = gy & 1
    barrier = pltpu.get_barrier_semaphore()

    def hello(m, carry):
        pl.semaphore_signal(
            barrier, inc=1, device_id=(gx ^ (m >> 4), gy ^ (m & 15)), device_id_type=MESH)
        return carry

    lax.fori_loop(1, 128, hello, 0)
    pl.semaphore_wait(barrier, 127)

    def copy(m):
        gx2, gy2 = gx ^ (m >> 4), gy ^ (m & 15)
        j = gx2 ^ (gy >> 1)
        return pltpu.make_async_remote_copy(
            src_ref=o.at[gy2, j], dst_ref=t.at[gx, j, half], send_sem=send.at[m],
            recv_sem=recv.at[m], device_id=(gx2, gy2), device_id_type=MESH)

    def start(m, carry):
        copy(m).start()
        return carry

    def finish(m, carry):
        copy(m).wait()
        return carry

    lax.fori_loop(1, 128, start, 0)
    j = gx ^ (gy >> 1)
    keep = pltpu.make_async_copy(o.at[gy, j], t.at[gx, j, half], here)
    keep.start()
    lax.fori_loop(1, 128, finish, 0)
    keep.wait()


def swap(o):
    return pl.pallas_call(
        swap_kernel,
        out_shape=jax.ShapeDtypeStruct((8, 8, 2, 2, 32, 128), BF16),
        in_specs=[ANY],
        out_specs=ANY,
        scratch_shapes=[pltpu.SemaphoreType.DMA((128,)), pltpu.SemaphoreType.DMA((128,)),
                        pltpu.SemaphoreType.DMA],
        compiler_params=pltpu.CompilerParams(collective_id=2, has_side_effects=True),
        name="swap",
    )(o.reshape(16, 8, 2, 32, 128))


def high_kernel(t_ref, v_ref, f_ref, state, turned):
    first = lax.broadcasted_iota(jnp.int32, (32, 128), 1) < 64
    for g in range(8):
        for half in range(2):
            tile = t_ref[g, 0, half, 0]
            state[0, g, :, half * 128:half * 128 + 128] = tile
            turned[0, g, :, half * 128:half * 128 + 128] = turn(tile.astype(F32), first)
    for level in range(3):
        now, later = level % 2, (level + 1) % 2
        for g in range(8):
            h = g ^ (1 << level)
            right = jnp.concatenate(
                [state[now, g], state[now, h], turned[now, g], turned[now, h]], axis=0)
            got = jnp.dot(v_ref[g, 0, level], right, preferred_element_type=F32)
            one, two = got[:, :128], got[:, 128:]
            if level == 2:
                f_ref[g, 0, 0] = jnp.where(first, one, pltpu.roll(two, 64, 1)).astype(BF16)
                f_ref[g, 0, 1] = jnp.where(first, pltpu.roll(one, 64, 1), two).astype(BF16)
            else:
                state[later, g] = got.astype(BF16)
                turned[later, g, :, :128] = turn(one, first)
                turned[later, g, :, 128:] = turn(two, first)


def high(t, v):
    return pl.pallas_call(
        high_kernel,
        grid=(16,),
        out_shape=jax.ShapeDtypeStruct((8, 16, 2, 32, 128), BF16),
        in_specs=[pl.BlockSpec((8, 1, 2, 1, 32, 128), lambda i: (0, i // 2, 0, i % 2, 0, 0)),
                  pl.BlockSpec((8, 1, 3, 32, 128), lambda i: (0, i // 2 + (i % 2) * 8, 0, 0, 0))],
        out_specs=pl.BlockSpec((8, 1, 2, 32, 128), lambda i: (0, i, 0, 0, 0)),
        scratch_shapes=[pltpu.VMEM((2, 8, 32, 256), BF16), pltpu.VMEM((2, 8, 32, 256), BF16)],
        compiler_params=pltpu.CompilerParams(vmem_limit_bytes=LIMIT),
        name="high",
    )(t, v)


def home_kernel(f, g, send, recv, here):
    gx, gy = place()
    greet([(gx ^ m, gy) for m in range(1, 8)])
    copies = [
        pltpu.make_async_remote_copy(
            src_ref=f.at[gx ^ m], dst_ref=g.at[gx], send_sem=send.at[m], recv_sem=recv.at[m],
            device_id=(gx ^ m, gy), device_id_type=MESH)
        for m in range(1, 8)]
    for copy in copies:
        copy.start()
    keep = pltpu.make_async_copy(f.at[gx], g.at[gx], here)
    keep.start()
    for copy in copies:
        copy.wait()
    keep.wait()


def home(f):
    return pl.pallas_call(
        home_kernel,
        out_shape=jax.ShapeDtypeStruct(f.shape, BF16),
        in_specs=[ANY],
        out_specs=ANY,
        scratch_shapes=[pltpu.SemaphoreType.DMA((8,)), pltpu.SemaphoreType.DMA((8,)),
                        pltpu.SemaphoreType.DMA],
        compiler_params=pltpu.CompilerParams(collective_id=3, has_side_effects=True),
        name="home",
    )(f)


def last_kernel(g_ref, e_ref, r_ref):
    j = pl.program_id(0) // 2
    table = jnp.concatenate([e_ref[0], -e_ref[1]], axis=0)
    for s in range(8):
        left = g_ref[s, 0].reshape(64, 128)
        got = lax.dot_general(
            left, table, (((0,), (0,)), ((), ())), preferred_element_type=F32)
        got = got.reshape(2, 8, 8, 128)
        for half in range(2):
            r_ref[:, 2 * (s ^ j) + half] = got[half]


def last(g, e):
    return pl.pallas_call(
        last_kernel,
        grid=(16,),
        out_shape=jax.ShapeDtypeStruct((8, 16, 8, 2048), F32),
        in_specs=[pl.BlockSpec((8, 1, 2, 32, 128), lambda i: (0, i, 0, 0, 0)),
                  pl.BlockSpec((2, 32, 128), lambda i: (0, 0, i // 2 + (i % 2) * 8))],
        out_specs=pl.BlockSpec((8, 16, 8, 128), lambda i: (0, 0, 0, i // 2 + (i % 2) * 8)),
        compiler_params=pltpu.CompilerParams(vmem_limit_bytes=LIMIT),
        name="last",
    )(g, e)


def on_device(samples, interp, translation, evaluate):
    by_box = samples.reshape(8, 2048, 128).transpose(1, 0, 2).reshape(8, 16, 16, 8, 128)
    levels = translation.transpose(2, 0, 3, 1, 4).reshape(16, 7, 32, 128)
    own_w = jnp.concatenate([interp.transpose(1, 0, 2, 3), levels[:, :4]], axis=1)
    own_v = levels[:, 4:]
    x, w, v = spread(by_box, own_w, own_v)
    state = home(high(swap(low(x, w)), v))
    return last(state, evaluate.transpose(0, 2, 1)).reshape(1024, 2048)


def solution(mesh):
    in_specs = (
        P(("gx", "gy"), None),
        P(None, ("gx", "gy"), None, None),
        P(None, None, ("gx", "gy"), None, None),
        P(None, ("gx", "gy"), None),
    )
    out_specs = P(None, ("gx", "gy"))
    return jax.shard_map(
        on_device, mesh=mesh, in_specs=in_specs, out_specs=out_specs, check_vma=False
    )
```

```python
import jax
import jax.numpy as jnp
from jax import lax
from jax.experimental import pallas as pl
from jax.experimental.pallas import tpu as pltpu
from jax.sharding import PartitionSpec as P

MESH = pl.DeviceIdType.MESH
F32, BF16 = jnp.float32, jnp.bfloat16
ANY = pl.BlockSpec(memory_space=pl.ANY)
LIMIT = 56 * 2**20


def place():
    return lax.axis_index("gx"), lax.axis_index("gy")


CHUNKS = 8
PAIR = 2


def target(gy, beta):
    c, y0, zh = gy & 1, (gy >> 1) & 1, gy >> 3
    return ((zh ^ beta) << 2) | (c << 1) | (y0 ^ beta)


def origin(gx, beta, half):
    return (((gx >> 2) ^ beta) << 3) | (half << 2) | (((gx & 1) ^ beta) << 1) | ((gx >> 1) & 1)


def boxes(k):
    return pl.ds(k * PAIR, PAIR)


def remote(src, dst, send, recv, device):
    return pltpu.make_async_remote_copy(
        src_ref=src, dst_ref=dst, send_sem=send, recv_sem=recv,
        device_id=device, device_id_type=MESH)


def drain(ref, sem):
    pltpu.make_async_copy(ref, ref, sem).wait()


def main_kernel(samples, interp, translation, g_ref,
                x, raw, w, v, o, t, f, low_state, low_turned, high_state, high_turned,
                x_recv, w_recv, v_recv, t_recv, sent, here):
    gx, gy = place()
    half = (gy >> 2) & 1
    far, core, mate = gy ^ 8, gy ^ 1, gx ^ 4
    x_sent, w_sent, v_sent, o_sent, f_sent, g_recv = [sent.at[i] for i in range(6)]
    own_target = [target(gy, beta) == gx for beta in range(2)]

    load = [pltpu.make_async_copy(translation, raw, here.at[0]),
            pltpu.make_async_copy(interp.at[0], w.at[gy, :, 0], here.at[1]),
            pltpu.make_async_copy(interp.at[1], w.at[gy, :, 1], here.at[2])]
    for copy in load:
        copy.start()

    barrier = pltpu.get_barrier_semaphore()

    def hello(device):
        pl.semaphore_signal(barrier, inc=1, device_id=device, device_id_type=MESH)

    for m in (1, 2, 4, 6, 8):
        hello((gx, gy ^ m))
    for m in range(1, 8):
        hello((gx ^ m, gy))
    for beta in range(2):
        for side in range(2):
            source = origin(gx, beta, side)
            for m in range(1, 8):
                hello((gx ^ m, source))

            @pl.when(source != gy)
            def _():
                hello((gx, source))
    selves = jnp.where(own_target[0], 1, 0) + jnp.where(own_target[1], 1, 0)
    pl.semaphore_wait(barrier, 12 + 32 - selves)

    def send_samples(k, carry):
        for m in range(1, 8):
            remote(samples.at[gx ^ m, :, boxes(k)], x.at[k, gx], x_sent, x_recv.at[k],
                   (gx ^ m, gy)).start()
        pltpu.make_async_copy(samples.at[gx, :, boxes(k)], x.at[k, gx], x_recv.at[k]).start()
        return carry

    lax.fori_loop(0, CHUNKS, send_samples, 0)

    for copy in load:
        copy.wait()

    def pack(b, carry):
        for level in range(7):
            pair = jnp.concatenate([raw[level, 0, b], raw[level, 1, b]], axis=1)
            if level < 4:
                w[gy, b, 2 + level] = pair
            else:
                v[gx, b, level - 4] = pair
        return carry

    lax.fori_loop(0, 16, pack, 0)

    def send_w(slot, k, flip, kind):
        remote(w.at[slot, boxes(k)], w.at[slot, boxes(k)], w_sent, w_recv.at[kind, k],
               (gx, gy ^ flip)).start()

    def got_w(k, kind):
        drain(w.at[0, boxes(k)], w_recv.at[kind, k])

    def own_w(k):
        send_w(gy, k, 8, 0)
        for i, m in enumerate((2, 4, 6)):
            send_w(gy, k, m, 1 + i)
        send_w(gy, k, 1, 7)

    def far_w(k):
        got_w(k, 0)
        for i, m in enumerate((2, 4, 6)):
            send_w(far, k, m, 4 + i)
        send_w(far, k, 1, 7)

    def core_w(k):
        for i, m in enumerate((2, 4, 6)):
            got_w(k, 1 + i)
            send_w(gy ^ m, k, 1, 7)
        for i, m in enumerate((2, 4, 6)):
            got_w(k, 4 + i)
            send_w(far ^ m, k, 1, 7)

    def send_v(slot, k, flip, kind):
        remote(v.at[slot, boxes(k)], v.at[slot, boxes(k)], v_sent, v_recv.at[kind, k],
               (gx ^ flip, gy)).start()

    def own_v(k):
        send_v(gx, k, 4, 0)
        for m in (1, 2, 3):
            send_v(gx, k, m, 1)

    def mate_v(k):
        drain(v.at[0, boxes(k)], v_recv.at[0, k])
        for m in (1, 2, 3):
            send_v(mate, k, m, 1)

    first = lax.broadcasted_iota(jnp.int32, (32, 128), 1) < 64

    def low(k):
        def one(beta, carry):
            b = k * PAIR + beta
            for g in range(16):
                rows = x[k, :, g, beta].reshape(64, 128)
                table = w[g, b, 0:2].reshape(64, 128)
                got = lax.dot_general(
                    table, rows, (((1,), (1,)), ((), ())), preferred_element_type=F32)
                pair = jnp.concatenate([got[:32], got[32:]], axis=1)
                low_state[0, g] = pair.astype(BF16)
                low_turned[0, g] = turn(pair, first)
            for level in range(4):
                now, later = level % 2, (level + 1) % 2
                for g in range(16):
                    h = g ^ (1 << level)
                    right = jnp.concatenate(
                        [low_state[now, g], low_state[now, h],
                         low_turned[now, g], low_turned[now, h]], axis=0)
                    got = jnp.dot(w[g, b, 2 + level], right, preferred_element_type=F32)
                    if level == 3:
                        o[g, b] = got.astype(BF16)
                    else:
                        low_state[later, g] = got.astype(BF16)
                        low_turned[later, g] = turn(got, first)
            return carry

        lax.fori_loop(0, PAIR, one, 0)

    def send_o(k):
        def each(i, carry):
            gy2 = gy ^ i ^ ((gx & 3) << 1) ^ ((gx >> 2) << 3)
            for beta in range(2):
                gx2 = target(gy, beta)
                src = o.at[gy2, k * PAIR + beta]
                dst = t.at[k, gx, half, beta]
                mine = (gx2 == gx) & (gy2 == gy)

                @pl.when(mine)
                def _():
                    pltpu.make_async_copy(src, dst, t_recv.at[k]).start()

                @pl.when(jnp.logical_not(mine))
                def _():
                    remote(src, dst, o_sent, t_recv.at[k], (gx2, gy2)).start()
            return carry

        lax.fori_loop(0, 16, each, 0)

    def high(k):
        def one(beta, carry):
            b = k * PAIR + beta
            for g in range(8):
                for side in range(2):
                    tile = t[k, g, side, beta]
                    high_state[0, g, :, side * 128:side * 128 + 128] = tile
                    high_turned[0, g, :, side * 128:side * 128 + 128] = turn(
                        tile.astype(F32), first)
            for level in range(3):
                now, later = level % 2, (level + 1) % 2
                for g in range(8):
                    h = g ^ (1 << level)
                    right = jnp.concatenate(
                        [high_state[now, g], high_state[now, h],
                         high_turned[now, g], high_turned[now, h]], axis=0)
                    got = jnp.dot(v[g, b, level], right, preferred_element_type=F32)
                    left, rest = got[:, :128], got[:, 128:]
                    if level == 2:
                        f[g, b, 0] = jnp.where(first, left, pltpu.roll(rest, 64, 1)).astype(BF16)
                        f[g, b, 1] = jnp.where(first, pltpu.roll(left, 64, 1), rest).astype(BF16)
                    else:
                        high_state[later, g] = got.astype(BF16)
                        high_turned[later, g, :, :128] = turn(left, first)
                        high_turned[later, g, :, 128:] = turn(rest, first)
            return carry

        lax.fori_loop(0, PAIR, one, 0)

    def send_f(k):
        for m in range(1, 8):
            remote(f.at[gx ^ m, boxes(k)], g_ref.at[gx, boxes(k)], f_sent, g_recv,
                   (gx ^ m, gy)).start()
        pltpu.make_async_copy(f.at[gx, boxes(k)], g_ref.at[gx, boxes(k)], g_recv).start()

    for k in range(3):
        own_w(k)
    far_w(0)
    far_w(1)
    core_w(0)
    own_v(0)

    def step(k, carry):
        @pl.when(k < CHUNKS - 3)
        def _():
            own_w(k + 3)

        @pl.when(k < CHUNKS - 1)
        def _():
            own_v(k + 1)

        @pl.when(k < CHUNKS - 2)
        def _():
            far_w(k + 2)

        @pl.when(k < CHUNKS - 1)
        def _():
            core_w(k + 1)

        @pl.when(k < CHUNKS)
        def _():
            mate_v(k)
            drain(w.at[pl.ds(0, 8), boxes(k)], w_recv.at[7, k])
            drain(x.at[k], x_recv.at[k])
            low(k)
            send_o(k)

        @pl.when(k > 0)
        def _():
            drain(v.at[pl.ds(0, 6), boxes(k - 1)], v_recv.at[1, k - 1])
            drain(t.at[k - 1], t_recv.at[k - 1])
            high(k - 1)
            send_f(k - 1)

        return carry

    lax.fori_loop(0, CHUNKS + 1, step, 0)
    drain(g_ref, g_recv)
    drain(f.at[pl.ds(0, 7)], f_sent)
    drain(x.at[:, pl.ds(0, 7)], x_sent)
    drain(w.at[pl.ds(0, 15)], w_sent)
    drain(v.at[pl.ds(0, 7)], v_sent)
    for beta in range(2):
        @pl.when(own_target[beta])
        def _():
            drain(o.at[pl.ds(0, 15), pl.ds(0, 8)], o_sent)

        @pl.when(jnp.logical_not(own_target[beta]))
        def _():
            drain(o.at[:, pl.ds(0, 8)], o_sent)


def main(samples, interp, translation):
    dma = pltpu.SemaphoreType.DMA
    return pl.pallas_call(
        main_kernel,
        out_shape=jax.ShapeDtypeStruct((8, 16, 2, 32, 128), BF16),
        in_specs=[ANY] * 3,
        out_specs=ANY,
        scratch_shapes=[
            pltpu.VMEM((CHUNKS, 8, 16, PAIR, 8, 128), BF16),
            pltpu.VMEM((7, 2, 16, 32, 64), BF16),
            pltpu.VMEM((16, 16, 6, 32, 128), BF16),
            pltpu.VMEM((8, 16, 3, 32, 128), BF16),
            pltpu.VMEM((16, 16, 32, 128), BF16),
            pltpu.VMEM((CHUNKS, 8, 2, PAIR, 32, 128), BF16),
            pltpu.VMEM((8, 16, 2, 32, 128), BF16),
            pltpu.VMEM((2, 16, 32, 128), BF16),
            pltpu.VMEM((2, 16, 32, 128), BF16),
            pltpu.VMEM((2, 8, 32, 256), BF16),
            pltpu.VMEM((2, 8, 32, 256), BF16),
            dma((CHUNKS,)), dma((8, CHUNKS)), dma((2, CHUNKS)), dma((CHUNKS,)), dma((6,)), dma((3,)),
        ],
        compiler_params=pltpu.CompilerParams(
            collective_id=1, has_side_effects=True, vmem_limit_bytes=LIMIT),
        cost_estimate=pl.CostEstimate(
            flops=2 * 2**30, bytes_accessed=10 * 2**20, transcendentals=0),
        name="levels",
    )(samples, interp, translation)


def turn(pair, first):
    moved = pltpu.roll(pair, 64, 1)
    return jnp.where(first, -moved, moved).astype(BF16)


def last_kernel(g_ref, e_ref, r_ref):
    beta = pl.program_id(0) % 2
    table = jnp.concatenate([e_ref[0], -e_ref[1]], axis=0)
    for s in range(8):
        left = g_ref[s, 0].reshape(64, 128)
        got = lax.dot_general(
            left, table, (((0,), (0,)), ((), ())), preferred_element_type=F32)
        got = got.reshape(2, 8, 8, 128)
        for half in range(2):
            r_ref[:, origin(s, beta, half)] = got[half]


def last(g, e):
    return pl.pallas_call(
        last_kernel,
        grid=(16,),
        out_shape=jax.ShapeDtypeStruct((8, 16, 8, 2048), F32),
        in_specs=[pl.BlockSpec((8, 1, 2, 32, 128), lambda b: (0, b, 0, 0, 0)),
                  pl.BlockSpec((2, 32, 128), lambda b: (0, 0, b))],
        out_specs=pl.BlockSpec((8, 16, 8, 128), lambda b: (0, 0, 0, b)),
        compiler_params=pltpu.CompilerParams(vmem_limit_bytes=LIMIT),
        name="last",
    )(g, e)


def on_device(samples, interp, translation, evaluate):
    by_box = samples.reshape(8, 2048, 128).transpose(1, 0, 2).reshape(8, 16, 16, 8, 128)
    state = main(by_box, interp, translation)
    return last(state, evaluate.transpose(0, 2, 1)).reshape(1024, 2048)


def solution(mesh):
    in_specs = (
        P(("gx", "gy"), None),
        P(None, ("gx", "gy"), None, None),
        P(None, None, ("gx", "gy"), None, None),
        P(None, ("gx", "gy"), None),
    )
    out_specs = P(None, ("gx", "gy"))
    return jax.shard_map(
        on_device, mesh=mesh, in_specs=in_specs, out_specs=out_specs, check_vma=False
    )
```

```python
import jax
import jax.numpy as jnp
from jax import lax
from jax.experimental import pallas as pl
from jax.experimental.pallas import tpu as pltpu
from jax.sharding import PartitionSpec as P

MESH = pl.DeviceIdType.MESH
F32, BF16 = jnp.float32, jnp.bfloat16
ANY = pl.BlockSpec(memory_space=pl.ANY)
LIMIT = 56 * 2**20


def place():
    return lax.axis_index("gx"), lax.axis_index("gy")


CHUNKS = 8
PAIR = 2


def target(gy, beta):
    c, y0, zh = gy & 1, (gy >> 1) & 1, gy >> 3
    return ((zh ^ beta) << 2) | (c << 1) | (y0 ^ beta)


def origin(gx, beta, half):
    return (((gx >> 2) ^ beta) << 3) | (half << 2) | (((gx & 1) ^ beta) << 1) | ((gx >> 1) & 1)


def boxes(k):
    return pl.ds(k * PAIR, PAIR)


def remote(src, dst, send, recv, device):
    return pltpu.make_async_remote_copy(
        src_ref=src, dst_ref=dst, send_sem=send, recv_sem=recv,
        device_id=device, device_id_type=MESH)


def drain(ref, sem):
    pltpu.make_async_copy(ref, ref, sem).wait()


def main_kernel(samples, interp, translation, g_ref,
                x, raw, w, v, o, t, f, low_state, low_turned, high_state, high_turned,
                x_recv, w_recv, v_recv, t_recv, sent, here):
    gx, gy = place()
    half = (gy >> 2) & 1
    far, core, mate = gy ^ 8, gy ^ 1, gx ^ 4
    x_sent, w_sent, v_sent, o_sent, f_sent, g_recv = [sent.at[i] for i in range(6)]
    own_target = [target(gy, beta) == gx for beta in range(2)]

    load = [pltpu.make_async_copy(translation, raw, here.at[0]),
            pltpu.make_async_copy(interp.at[0], w.at[gy, :, 0], here.at[1]),
            pltpu.make_async_copy(interp.at[1], w.at[gy, :, 1], here.at[2])]
    for copy in load:
        copy.start()

    barrier = pltpu.get_barrier_semaphore()

    def hello(device):
        pl.semaphore_signal(barrier, inc=1, device_id=device, device_id_type=MESH)

    for m in (1, 2, 4, 6, 8):
        hello((gx, gy ^ m))
    for m in range(1, 8):
        hello((gx ^ m, gy))
    for beta in range(2):
        for side in range(2):
            source = origin(gx, beta, side)
            for m in range(1, 8):
                hello((gx ^ m, source))

            @pl.when(source != gy)
            def _():
                hello((gx, source))
    selves = jnp.where(own_target[0], 1, 0) + jnp.where(own_target[1], 1, 0)
    pl.semaphore_wait(barrier, 12 + 32 - selves)

    def send_samples(k, carry):
        for m in range(1, 8):
            remote(samples.at[gx ^ m, :, boxes(k)], x.at[k, gx], x_sent, x_recv.at[k],
                   (gx ^ m, gy)).start()
        pltpu.make_async_copy(samples.at[gx, :, boxes(k)], x.at[k, gx], x_recv.at[k]).start()
        return carry

    lax.fori_loop(0, CHUNKS, send_samples, 0)

    for copy in load:
        copy.wait()

    low_half = lax.broadcasted_iota(jnp.int32, (32, 128), 1) % 64 < 32

    def pack(b, carry):
        for level in range(7):
            pair = jnp.concatenate([raw[level, 0, b], raw[level, 1, b]], axis=1)
            bit = (gy >> level) & 1 if level < 4 else (gx >> (level - 4)) & 1
            wide = pair.astype(F32)
            other = jnp.where(low_half, pltpu.roll(wide, 96, 1), pltpu.roll(wide, 32, 1))
            pair = jnp.where(bit == 1, other, wide).astype(BF16)
            if level < 4:
                w[gy, b, 2 + level] = pair
            else:
                v[gx, b, level - 4] = pair
        return carry

    lax.fori_loop(0, 16, pack, 0)

    def send_w(slot, k, flip, kind):
        remote(w.at[slot, boxes(k)], w.at[slot, boxes(k)], w_sent, w_recv.at[kind, k],
               (gx, gy ^ flip)).start()

    def got_w(k, kind):
        drain(w.at[0, boxes(k)], w_recv.at[kind, k])

    def own_w(k):
        send_w(gy, k, 8, 0)
        for i, m in enumerate((2, 4, 6)):
            send_w(gy, k, m, 1 + i)
        send_w(gy, k, 1, 7)

    def far_w(k):
        got_w(k, 0)
        for i, m in enumerate((2, 4, 6)):
            send_w(far, k, m, 4 + i)
        send_w(far, k, 1, 7)

    def core_w(k):
        for i, m in enumerate((2, 4, 6)):
            got_w(k, 1 + i)
            send_w(gy ^ m, k, 1, 7)
        for i, m in enumerate((2, 4, 6)):
            got_w(k, 4 + i)
            send_w(far ^ m, k, 1, 7)

    def send_v(slot, k, flip, kind):
        remote(v.at[slot, boxes(k)], v.at[slot, boxes(k)], v_sent, v_recv.at[kind, k],
               (gx ^ flip, gy)).start()

    def own_v(k):
        send_v(gx, k, 4, 0)
        for m in (1, 2, 3):
            send_v(gx, k, m, 1)

    def mate_v(k):
        drain(v.at[0, boxes(k)], v_recv.at[0, k])
        for m in (1, 2, 3):
            send_v(mate, k, m, 1)

    first = lax.broadcasted_iota(jnp.int32, (32, 128), 1) < 64

    def low(k):
        def box_of(beta, carry):
            b = k * PAIR + beta
            for g in range(16):
                rows = x[k, :, g, beta].reshape(64, 128)
                table = w[g, b, 0:2].reshape(64, 128)
                got = lax.dot_general(
                    table, rows, (((1,), (1,)), ((), ())), preferred_element_type=F32)
                pair = jnp.concatenate([got[:32], got[32:]], axis=1)
                low_state[0, g] = pair.astype(BF16)
                low_turned[0, g] = turn(pair, first)
            for level in range(4):
                now, later = level % 2, (level + 1) % 2
                for g in range(16):
                    h = g ^ (1 << level)
                    if h < g:
                        continue
                    right = jnp.concatenate(
                        [low_state[now, g], low_state[now, h],
                         low_turned[now, g], low_turned[now, h]], axis=0)
                    left = jnp.concatenate([w[g, b, 2 + level], w[h, b, 2 + level]], axis=0)
                    both = jnp.dot(left, right, preferred_element_type=F32)
                    for box, got in ((g, both[:32]), (h, both[32:])):
                        if level == 3:
                            o[box, b] = got.astype(BF16)
                        else:
                            low_state[later, box] = got.astype(BF16)
                            low_turned[later, box] = turn(got, first)
            return carry

        lax.fori_loop(0, PAIR, box_of, 0)

    def send_o(k):
        def each(i, carry):
            gy2 = gy ^ i ^ ((gx & 3) << 1) ^ ((gx >> 2) << 3)
            for beta in range(2):
                gx2 = target(gy, beta)
                src = o.at[gy2, k * PAIR + beta]
                dst = t.at[k, gx, half, beta]
                mine = (gx2 == gx) & (gy2 == gy)

                @pl.when(mine)
                def _():
                    pltpu.make_async_copy(src, dst, t_recv.at[k]).start()

                @pl.when(jnp.logical_not(mine))
                def _():
                    remote(src, dst, o_sent, t_recv.at[k], (gx2, gy2)).start()
            return carry

        lax.fori_loop(0, 16, each, 0)

    def high(k):
        def box_of(beta, carry):
            b = k * PAIR + beta
            for g in range(8):
                for side in range(2):
                    tile = t[k, g, side, beta]
                    high_state[0, g, :, side * 128:side * 128 + 128] = tile
                    high_turned[0, g, :, side * 128:side * 128 + 128] = turn(
                        tile.astype(F32), first)
            for level in range(3):
                now, later = level % 2, (level + 1) % 2
                for g in range(8):
                    h = g ^ (1 << level)
                    if h < g:
                        continue
                    right = jnp.concatenate(
                        [high_state[now, g], high_state[now, h],
                         high_turned[now, g], high_turned[now, h]], axis=0)
                    left = jnp.concatenate([v[g, b, level], v[h, b, level]], axis=0)
                    both = jnp.dot(left, right, preferred_element_type=F32)
                    for box, got in ((g, both[:32]), (h, both[32:])):
                        one, two = got[:, :128], got[:, 128:]
                        if level == 2:
                            f[box, b, 0] = jnp.where(
                                first, one, pltpu.roll(two, 64, 1)).astype(BF16)
                            f[box, b, 1] = jnp.where(
                                first, pltpu.roll(one, 64, 1), two).astype(BF16)
                        else:
                            high_state[later, box] = got.astype(BF16)
                            high_turned[later, box, :, :128] = turn(one, first)
                            high_turned[later, box, :, 128:] = turn(two, first)
            return carry

        lax.fori_loop(0, PAIR, box_of, 0)

    def send_f(k):
        for m in range(1, 8):
            remote(f.at[gx ^ m, boxes(k)], g_ref.at[gx, boxes(k)], f_sent, g_recv,
                   (gx ^ m, gy)).start()
        pltpu.make_async_copy(f.at[gx, boxes(k)], g_ref.at[gx, boxes(k)], g_recv).start()

    def upto(n, fn):
        lax.fori_loop(0, n, lambda k, c: (fn(k), c)[1], 0)

    upto(8, own_w)
    upto(8, own_v)
    upto(4, far_w)
    upto(2, core_w)
    upto(1, mate_v)

    def ahead(k, by, fn):
        @pl.when(k + by < CHUNKS)
        def _():
            fn(k + by)

    def relays(k):
        ahead(k, 4, far_w)
        ahead(k, 2, core_w)
        ahead(k, 1, mate_v)

    def step(k, carry):
        pass

        @pl.when(k < CHUNKS)
        def _():
            drain(w.at[pl.ds(0, 8), boxes(k)], w_recv.at[7, k])
            drain(x.at[k], x_recv.at[k])
            low(k)
            send_o(k)

        relays(k)

        @pl.when(k > 0)
        def _():
            drain(v.at[pl.ds(0, 6), boxes(k - 1)], v_recv.at[1, k - 1])
            drain(t.at[k - 1], t_recv.at[k - 1])
            high(k - 1)
            send_f(k - 1)

        return carry

    lax.fori_loop(0, CHUNKS + 1, step, 0)
    drain(g_ref, g_recv)
    drain(f.at[pl.ds(0, 7)], f_sent)
    drain(x.at[:, pl.ds(0, 7)], x_sent)
    drain(w.at[pl.ds(0, 15)], w_sent)
    drain(v.at[pl.ds(0, 7)], v_sent)
    for beta in range(2):
        @pl.when(own_target[beta])
        def _():
            drain(o.at[pl.ds(0, 15), pl.ds(0, 8)], o_sent)

        @pl.when(jnp.logical_not(own_target[beta]))
        def _():
            drain(o.at[:, pl.ds(0, 8)], o_sent)


def main(samples, interp, translation):
    dma = pltpu.SemaphoreType.DMA
    return pl.pallas_call(
        main_kernel,
        out_shape=jax.ShapeDtypeStruct((8, 16, 2, 32, 128), BF16),
        in_specs=[ANY] * 3,
        out_specs=ANY,
        scratch_shapes=[
            pltpu.VMEM((CHUNKS, 8, 16, PAIR, 8, 128), BF16),
            pltpu.VMEM((7, 2, 16, 32, 64), BF16),
            pltpu.VMEM((16, 16, 6, 32, 128), BF16),
            pltpu.VMEM((8, 16, 3, 32, 128), BF16),
            pltpu.VMEM((16, 16, 32, 128), BF16),
            pltpu.VMEM((CHUNKS, 8, 2, PAIR, 32, 128), BF16),
            pltpu.VMEM((8, 16, 2, 32, 128), BF16),
            pltpu.VMEM((2, 16, 32, 128), BF16),
            pltpu.VMEM((2, 16, 32, 128), BF16),
            pltpu.VMEM((2, 8, 32, 256), BF16),
            pltpu.VMEM((2, 8, 32, 256), BF16),
            dma((CHUNKS,)), dma((8, CHUNKS)), dma((2, CHUNKS)), dma((CHUNKS,)), dma((6,)), dma((3,)),
        ],
        compiler_params=pltpu.CompilerParams(
            collective_id=1, has_side_effects=True, vmem_limit_bytes=LIMIT),
        cost_estimate=pl.CostEstimate(
            flops=2 * 2**30, bytes_accessed=10 * 2**20, transcendentals=0),
        name="levels",
    )(samples, interp, translation)


def turn(pair, first):
    moved = pltpu.roll(pair, 64, 1)
    return jnp.where(first, -moved, moved).astype(BF16)


def last_kernel(g_ref, e_ref, r_ref):
    table = jnp.concatenate([e_ref[0], -e_ref[1]], axis=0)
    none = jnp.zeros((64, 128), BF16)
    table = jnp.concatenate(
        [jnp.concatenate([table[:, :128], none], axis=1),
         jnp.concatenate([none, table[:, 128:]], axis=1)], axis=0)
    for s in range(8):
        left = g_ref[s].reshape(128, 128)
        got = lax.dot_general(
            left, table, (((0,), (0,)), ((), ())), preferred_element_type=F32)
        got = got.reshape(2, 8, 8, 256)
        for beta in range(PAIR):
            lanes = slice(beta * 128, beta * 128 + 128)
            for half in range(2):
                r_ref[:, origin(s, beta, half), :, lanes] = got[half, :, :, lanes]


def last(g, e):
    return pl.pallas_call(
        last_kernel,
        grid=(CHUNKS,),
        out_shape=jax.ShapeDtypeStruct((8, 16, 8, 2048), F32),
        in_specs=[pl.BlockSpec((8, PAIR, 2, 32, 128), lambda k: (0, k, 0, 0, 0)),
                  pl.BlockSpec((2, 32, 256), lambda k: (0, 0, k))],
        out_specs=pl.BlockSpec((8, 16, 8, 256), lambda k: (0, 0, 0, k)),
        compiler_params=pltpu.CompilerParams(vmem_limit_bytes=LIMIT),
        name="last",
    )(g, e)


def on_device(samples, interp, translation, evaluate):
    by_box = samples.reshape(8, 2048, 128).transpose(1, 0, 2).reshape(8, 16, 16, 8, 128)
    state = main(by_box, interp, translation)
    return last(state, evaluate.transpose(0, 2, 1)).reshape(1024, 2048)


def solution(mesh):
    in_specs = (
        P(("gx", "gy"), None),
        P(None, ("gx", "gy"), None, None),
        P(None, None, ("gx", "gy"), None, None),
        P(None, ("gx", "gy"), None),
    )
    out_specs = P(None, ("gx", "gy"))
    return jax.shard_map(
        on_device, mesh=mesh, in_specs=in_specs, out_specs=out_specs, check_vma=False
    )
```

```python
import jax
import jax.numpy as jnp
from jax import lax
from jax.experimental import pallas as pl
from jax.experimental.pallas import tpu as pltpu
from jax.sharding import PartitionSpec as P

MESH = pl.DeviceIdType.MESH
F32, BF16 = jnp.float32, jnp.bfloat16
ANY = pl.BlockSpec(memory_space=pl.ANY)
LIMIT = 56 * 2**20


def place():
    return lax.axis_index("gx"), lax.axis_index("gy")


CHUNKS = 8
PAIR = 2


def target(gy, beta):
    c, y0, zh = gy & 1, (gy >> 1) & 1, gy >> 3
    return ((zh ^ beta) << 2) | (c << 1) | (y0 ^ beta)


def origin(gx, beta, half):
    return (((gx >> 2) ^ beta) << 3) | (half << 2) | (((gx & 1) ^ beta) << 1) | ((gx >> 1) & 1)


def boxes(k):
    return pl.ds(k * PAIR, PAIR)


def remote(src, dst, send, recv, device):
    return pltpu.make_async_remote_copy(
        src_ref=src, dst_ref=dst, send_sem=send, recv_sem=recv,
        device_id=device, device_id_type=MESH)


def drain(ref, sem):
    pltpu.make_async_copy(ref, ref, sem).wait()


def main_kernel(samples, interp, translation, g_ref,
                x, raw, w, v, o, t, f, low_state, low_turned, high_state, high_turned,
                x_recv, w_recv, v_recv, t_recv, sent, here):
    gx, gy = place()
    half = (gy >> 2) & 1
    x_up = (gx & 4) | ((gx + 1) & 3)
    x_down = (gx & 4) | ((gx + 3) & 3)
    far, core, mate = gy ^ 8, gy ^ 1, gx ^ 4
    x_sent, w_sent, v_sent, o_sent, f_sent, g_recv = [sent.at[i] for i in range(6)]
    own_target = [target(gy, beta) == gx for beta in range(2)]

    load = [pltpu.make_async_copy(translation, raw, here.at[0]),
            pltpu.make_async_copy(interp.at[0], w.at[gy, :, 0], here.at[1]),
            pltpu.make_async_copy(interp.at[1], w.at[gy, :, 1], here.at[2])]
    for copy in load:
        copy.start()

    barrier = pltpu.get_barrier_semaphore()

    def hello(device):
        pl.semaphore_signal(barrier, inc=1, device_id=device, device_id_type=MESH)

    for m in (1, 2, 4, 6, 8):
        hello((gx, gy ^ m))
    for m in range(1, 8):
        hello((gx ^ m, gy))
    for beta in range(2):
        for side in range(2):
            source = origin(gx, beta, side)
            for m in range(1, 8):
                hello((gx ^ m, source))

            @pl.when(source != gy)
            def _():
                hello((gx, source))
    selves = jnp.where(own_target[0], 1, 0) + jnp.where(own_target[1], 1, 0)
    pl.semaphore_wait(barrier, 12 + 32 - selves)

    def send_samples(k, carry):
        for m in range(1, 8):
            remote(samples.at[gx ^ m, :, boxes(k)], x.at[k, gx], x_sent, x_recv.at[k],
                   (gx ^ m, gy)).start()
        pltpu.make_async_copy(samples.at[gx, :, boxes(k)], x.at[k, gx], x_recv.at[k]).start()
        return carry

    lax.fori_loop(0, 2, send_samples, 0)

    for copy in load:
        copy.wait()

    low_half = lax.broadcasted_iota(jnp.int32, (32, 128), 1) % 64 < 32

    def pack(b, carry):
        for level in range(7):
            pair = jnp.concatenate([raw[level, 0, b], raw[level, 1, b]], axis=1)
            bit = (gy >> level) & 1 if level < 4 else (gx >> (level - 4)) & 1
            wide = pair.astype(F32)
            other = jnp.where(low_half, pltpu.roll(wide, 96, 1), pltpu.roll(wide, 32, 1))
            pair = jnp.where(bit == 1, other, wide).astype(BF16)
            if level < 4:
                w[gy, b, 2 + level] = pair
            else:
                v[gx, b, level - 4] = pair
        return carry

    lax.fori_loop(0, 16, pack, 0)

    def send_w(slot, k, flip, kind):
        remote(w.at[slot, boxes(k)], w.at[slot, boxes(k)], w_sent, w_recv.at[kind, k],
               (gx, gy ^ flip)).start()

    def got_w(k, kind):
        drain(w.at[0, boxes(k)], w_recv.at[kind, k])

    def own_w(k):
        send_w(gy, k, 8, 0)
        for i, m in enumerate((2, 4, 6)):
            send_w(gy, k, m, 1 + i)
        send_w(gy, k, 1, 7)

    def far_w(k):
        got_w(k, 0)
        for i, m in enumerate((2, 4, 6)):
            send_w(far, k, m, 4 + i)
        send_w(far, k, 1, 7)

    def core_w(k):
        for i, m in enumerate((2, 4, 6)):
            got_w(k, 1 + i)
            send_w(gy ^ m, k, 1, 7)
        for i, m in enumerate((2, 4, 6)):
            got_w(k, 4 + i)
            send_w(far ^ m, k, 1, 7)

    def send_v(slot, j, part, to, kind):
        rows = (pl.ds(j * 4, 2), pl.ds(j * 4 + 2, 2), pl.ds(j * 4, 4))[part]
        remote(v.at[slot, rows], v.at[slot, rows], v_sent, v_recv.at[kind, j], (to, gy)).start()

    def got_v(j, kind):
        drain(v.at[0, pl.ds(j * 4, 4)], v_recv.at[kind, j])

    def own_v(j):
        send_v(gx, j, 2, mate, 0)
        send_v(gx, j, 2, x_up, 1)
        send_v(gx, j, 2, x_down, 2)

    def mate_v(j):
        got_v(j, 0)
        send_v(mate, j, 2, x_up, 3)
        send_v(mate, j, 2, x_down, 4)

    def relay_v(j, flip, kind):
        got_v(j, kind)
        send_v(x_down ^ flip, j, 0, x_up, 5)
        got_v(j, kind + 1)
        send_v(x_up ^ flip, j, 1, x_down, 5)

    def drain_v(k):
        @pl.when(k % 2 == 0)
        def _():
            drain(v.at[pl.ds(0, 2), pl.ds((k // 2) * 4, 4)], v_recv.at[5, k // 2])

    first = lax.broadcasted_iota(jnp.int32, (32, 128), 1) < 64

    def low(k):
        def box_of(beta, carry):
            b = k * PAIR + beta
            for g in range(16):
                rows = x[k, :, g, beta].reshape(64, 128)
                table = w[g, b, 0:2].reshape(64, 128)
                got = lax.dot_general(
                    table, rows, (((1,), (1,)), ((), ())), preferred_element_type=F32)
                pair = jnp.concatenate([got[:32], got[32:]], axis=1)
                low_state[0, g] = pair.astype(BF16)
                low_turned[0, g] = turn(pair, first)
            for level in range(4):
                now, later = level % 2, (level + 1) % 2
                for g in range(16):
                    h = g ^ (1 << level)
                    if h < g:
                        continue
                    right = jnp.concatenate(
                        [low_state[now, g], low_state[now, h],
                         low_turned[now, g], low_turned[now, h]], axis=0)
                    left = jnp.concatenate([w[g, b, 2 + level], w[h, b, 2 + level]], axis=0)
                    both = jnp.dot(left, right, preferred_element_type=F32)
                    for box, got in ((g, both[:32]), (h, both[32:])):
                        if level == 3:
                            o[box, b] = got.astype(BF16)
                        else:
                            low_state[later, box] = got.astype(BF16)
                            low_turned[later, box] = turn(got, first)
            return carry

        lax.fori_loop(0, PAIR, box_of, 0)

    def send_o(k):
        def each(i, carry):
            gy2 = gy ^ i ^ ((gx & 3) << 1) ^ ((gx >> 2) << 3)
            for beta in range(2):
                gx2 = target(gy, beta)
                src = o.at[gy2, k * PAIR + beta]
                dst = t.at[k, gx, half, beta]
                mine = (gx2 == gx) & (gy2 == gy)

                @pl.when(mine)
                def _():
                    pltpu.make_async_copy(src, dst, t_recv.at[k]).start()

                @pl.when(jnp.logical_not(mine))
                def _():
                    remote(src, dst, o_sent, t_recv.at[k], (gx2, gy2)).start()
            return carry

        lax.fori_loop(0, 16, each, 0)

    def high(k):
        def box_of(beta, carry):
            b = k * PAIR + beta
            for g in range(8):
                for side in range(2):
                    tile = t[k, g, side, beta]
                    high_state[0, g, :, side * 128:side * 128 + 128] = tile
                    high_turned[0, g, :, side * 128:side * 128 + 128] = turn(
                        tile.astype(F32), first)
            for level in range(3):
                now, later = level % 2, (level + 1) % 2
                for g in range(8):
                    h = g ^ (1 << level)
                    if h < g:
                        continue
                    right = jnp.concatenate(
                        [high_state[now, g], high_state[now, h],
                         high_turned[now, g], high_turned[now, h]], axis=0)
                    left = jnp.concatenate([v[g, b, level], v[h, b, level]], axis=0)
                    both = jnp.dot(left, right, preferred_element_type=F32)
                    for box, got in ((g, both[:32]), (h, both[32:])):
                        one, two = got[:, :128], got[:, 128:]
                        if level == 2:
                            f[box, b, 0] = jnp.where(
                                first, one, pltpu.roll(two, 64, 1)).astype(BF16)
                            f[box, b, 1] = jnp.where(
                                first, pltpu.roll(one, 64, 1), two).astype(BF16)
                        else:
                            high_state[later, box] = got.astype(BF16)
                            high_turned[later, box, :, :128] = turn(one, first)
                            high_turned[later, box, :, 128:] = turn(two, first)
            return carry

        lax.fori_loop(0, PAIR, box_of, 0)

    def send_f(k):
        for m in range(1, 8):
            remote(f.at[gx ^ m, boxes(k)], g_ref.at[gx, boxes(k)], f_sent, g_recv,
                   (gx ^ m, gy)).start()
        pltpu.make_async_copy(f.at[gx, boxes(k)], g_ref.at[gx, boxes(k)], g_recv).start()

    def upto(n, fn):
        lax.fori_loop(0, n, lambda k, c: (fn(k), c)[1], 0)

    upto(8, own_w)
    upto(4, own_v)
    lax.fori_loop(2, CHUNKS, send_samples, 0)
    upto(4, far_w)
    upto(2, core_w)

    def ahead(k, by, fn):
        @pl.when(k + by < CHUNKS)
        def _():
            fn(k + by)

    def relays(k):
        ahead(k, 4, far_w)
        ahead(k, 2, core_w)

        @pl.when(k < 4)
        def _():
            relay_v(k, 0, 1)
            mate_v(k)

        @pl.when((k > 0) & (k < 5))
        def _():
            relay_v(k - 1, 4, 3)

    def step(k, carry):
        pass

        @pl.when(k < CHUNKS)
        def _():
            drain(w.at[pl.ds(0, 8), boxes(k)], w_recv.at[7, k])
            drain(x.at[k], x_recv.at[k])
            low(k)
            send_o(k)

        relays(k)

        @pl.when(k >= 3)
        def _():
            drain_v(k - 3)
            drain(t.at[k - 3], t_recv.at[k - 3])
            high(k - 3)
            send_f(k - 3)

        return carry

    lax.fori_loop(0, CHUNKS + 3, step, 0)
    drain(g_ref, g_recv)
    drain(f.at[pl.ds(0, 7)], f_sent)
    drain(x.at[:, pl.ds(0, 7)], x_sent)
    drain(w.at[pl.ds(0, 15)], w_sent)
    drain(v.at[pl.ds(0, 7)], v_sent)
    for beta in range(2):
        @pl.when(own_target[beta])
        def _():
            drain(o.at[pl.ds(0, 15), pl.ds(0, 8)], o_sent)

        @pl.when(jnp.logical_not(own_target[beta]))
        def _():
            drain(o.at[:, pl.ds(0, 8)], o_sent)


def main(samples, interp, translation):
    dma = pltpu.SemaphoreType.DMA
    return pl.pallas_call(
        main_kernel,
        out_shape=jax.ShapeDtypeStruct((8, 16, 2, 32, 128), BF16),
        in_specs=[ANY] * 3,
        out_specs=ANY,
        scratch_shapes=[
            pltpu.VMEM((CHUNKS, 8, 16, PAIR, 8, 128), BF16),
            pltpu.VMEM((7, 2, 16, 32, 64), BF16),
            pltpu.VMEM((16, 16, 6, 32, 128), BF16),
            pltpu.VMEM((8, 16, 3, 32, 128), BF16),
            pltpu.VMEM((16, 16, 32, 128), BF16),
            pltpu.VMEM((CHUNKS, 8, 2, PAIR, 32, 128), BF16),
            pltpu.VMEM((8, 16, 2, 32, 128), BF16),
            pltpu.VMEM((2, 16, 32, 128), BF16),
            pltpu.VMEM((2, 16, 32, 128), BF16),
            pltpu.VMEM((2, 8, 32, 256), BF16),
            pltpu.VMEM((2, 8, 32, 256), BF16),
            dma((CHUNKS,)), dma((8, CHUNKS)), dma((6, 4)), dma((CHUNKS,)), dma((6,)), dma((3,)),
        ],
        compiler_params=pltpu.CompilerParams(
            collective_id=1, has_side_effects=True, vmem_limit_bytes=LIMIT),
        cost_estimate=pl.CostEstimate(
            flops=2 * 2**30, bytes_accessed=10 * 2**20, transcendentals=0),
        name="levels",
    )(samples, interp, translation)


def turn(pair, first):
    moved = pltpu.roll(pair, 64, 1)
    return jnp.where(first, -moved, moved).astype(BF16)


def last_kernel(g_ref, e_ref, r_ref, g, r, load, store):
    loads = [pltpu.make_async_copy(g_ref.at[:, boxes(k)], g.at[:, boxes(k)], load.at[k])
             for k in range(CHUNKS)]
    for copy in loads:
        copy.start()
    table = jnp.concatenate([e_ref[0], -e_ref[1]], axis=0)
    none = jnp.zeros((64, 128), BF16)
    stores = []
    for k in range(CHUNKS):
        at = k * 256
        pair = jnp.concatenate(
            [jnp.concatenate([table[:, at:at + 128], none], axis=1),
             jnp.concatenate([none, table[:, at + 128:at + 256]], axis=1)], axis=0)
        loads[k].wait()
        for s in range(8):
            left = g[s, k * PAIR:k * PAIR + PAIR].reshape(128, 128)
            got = lax.dot_general(
                left, pair, (((0,), (0,)), ((), ())), preferred_element_type=F32)
            got = got.reshape(2, 8, 8, 256)
            for beta in range(PAIR):
                lanes = slice(beta * 128, beta * 128 + 128)
                for half in range(2):
                    r[:, origin(s, beta, half), :, at + lanes.start:at + lanes.stop] = (
                        got[half, :, :, lanes])
        if k % 2 == 1:
            wide = pl.ds(at - 256, 512)
            copy = pltpu.make_async_copy(
                r.at[:, :, :, wide], r_ref.at[:, :, :, wide], store.at[k // 2])
            copy.start()
            stores.append(copy)
    for copy in stores:
        copy.wait()


def last(g, e):
    dma = pltpu.SemaphoreType.DMA
    return pl.pallas_call(
        last_kernel,
        out_shape=jax.ShapeDtypeStruct((8, 16, 8, 2048), F32),
        in_specs=[ANY, pl.BlockSpec(memory_space=pltpu.VMEM)],
        out_specs=ANY,
        scratch_shapes=[pltpu.VMEM(g.shape, BF16), pltpu.VMEM((8, 16, 8, 2048), F32),
                        dma((CHUNKS,)), dma((CHUNKS // 2,))],
        compiler_params=pltpu.CompilerParams(vmem_limit_bytes=LIMIT),
        name="last",
    )(g, e)


def on_device(samples, interp, translation, evaluate):
    by_box = samples.reshape(8, 2048, 128).transpose(1, 0, 2).reshape(8, 16, 16, 8, 128)
    state = main(by_box, interp, translation)
    return last(state, evaluate.transpose(0, 2, 1)).reshape(1024, 2048)


def solution(mesh):
    in_specs = (
        P(("gx", "gy"), None),
        P(None, ("gx", "gy"), None, None),
        P(None, None, ("gx", "gy"), None, None),
        P(None, ("gx", "gy"), None),
    )
    out_specs = P(None, ("gx", "gy"))
    return jax.shard_map(
        on_device, mesh=mesh, in_specs=in_specs, out_specs=out_specs, check_vma=False
    )
```

```python
import jax
import jax.numpy as jnp
from jax import lax
from jax.experimental import pallas as pl
from jax.experimental.pallas import tpu as pltpu
from jax.sharding import PartitionSpec as P

MESH = pl.DeviceIdType.MESH
F32, BF16 = jnp.float32, jnp.bfloat16
ANY = pl.BlockSpec(memory_space=pl.ANY)
LIMIT = 56 * 2**20


def place():
    return lax.axis_index("gx"), lax.axis_index("gy")


PARTS = 4


def block_of(q, y):
    return ((q >> 1) << 3) | (y << 1) | (q & 1)


def z_of(q):
    return (q >> 1) ^ (q & 1)


def q_of(z, e):
    return z if e == 0 else 3 - z


def remote(src, dst, send, recv, device):
    return pltpu.make_async_remote_copy(
        src_ref=src, dst_ref=dst, send_sem=send, recv_sem=recv,
        device_id=device, device_id_type=MESH)


def drain(ref, sem):
    pltpu.make_async_copy(ref, ref, sem).wait()


def main_kernel(samples, interp, translation, g_ref,
                x, raw, own_w, own_v, w, v, o, t, f, low_state, low_turned, high_state, high_turned,
                x_recv, w_recv, t_recv, sent, here):
    gx, gy = place()
    across, zl = gx & 3, gx >> 2
    y, q = (gy >> 1) & 3, ((gy >> 3) << 1) | (gy & 1)
    x_sent, w_sent, pass_sent, v_sent, o_sent, f_sent, v_recv, g_recv = [sent.at[i] for i in range(8)]
    own_z = z_of(q) == zl

    load = [pltpu.make_async_copy(translation, raw, here.at[0]),
            pltpu.make_async_copy(interp.at[0], own_w.at[:, 0], here.at[1]),
            pltpu.make_async_copy(interp.at[1], own_w.at[:, 1], here.at[2])]
    for copy in load:
        copy.start()

    barrier = pltpu.get_barrier_semaphore()

    def hello(device):
        pl.semaphore_signal(barrier, inc=1, device_id=device, device_id_type=MESH)

    def hello_samples(i, carry):
        hello((gx ^ (i & 7), block_of(q ^ (i >> 3), y)))
        return carry

    lax.fori_loop(1, 32, hello_samples, 0)
    for m in (1, 2, 3):
        hello((gx, block_of(q, y ^ m)))
    for e in range(2):
        source_q = q_of(zl, e)

        def hello_state(i, carry):
            gx1, gy1 = i & 7, block_of(source_q, i >> 3)

            @pl.when((gx1 != gx) | (gy1 != gy))
            def _():
                hello((gx1, gy1))
            return carry

        lax.fori_loop(0, 32, hello_state, 0)

    for copy in load:
        copy.wait()
    low_half = lax.broadcasted_iota(jnp.int32, (32, 128), 1) % 64 < 32

    def pack(b, carry):
        for level in range(7):
            pair = jnp.concatenate([raw[level, 0, b], raw[level, 1, b]], axis=1)
            bit = (gy >> level) & 1 if level < 4 else (gx >> (level - 4)) & 1
            wide = pair.astype(F32)
            other = jnp.where(low_half, pltpu.roll(wide, 96, 1), pltpu.roll(wide, 32, 1))
            pair = jnp.where(bit == 1, other, wide).astype(BF16)
            if level < 4:
                own_w[b, 2 + level] = pair
            else:
                own_v[b, level - 4] = pair
        return carry

    lax.fori_loop(0, 16, pack, 0)
    pl.semaphore_wait(barrier, 31 + 3 + 64 - jnp.where(own_z, 1, 0))

    def send_samples(part, those=range(8)):
        to = block_of(q ^ part, y)
        for m in those:
            src = samples.at[gx ^ m, :, pl.ds((q ^ part) * 4, 4)]
            if m == 0 and part == 0:
                pltpu.make_async_copy(src, x.at[part, gx], x_recv.at[part]).start()
            else:
                remote(src, x.at[part, gx], x_sent, x_recv.at[part], (gx ^ m, to)).start()

    def own(i):
        beta = i ^ across
        for m in range(4):
            src, dst = own_w.at[(q ^ m) * 4 + beta], w.at[beta, y, q]
            if m == 0:
                pltpu.make_async_copy(src, dst, w_recv.at[0, i]).start()
            else:
                remote(src, dst, w_sent, w_recv.at[0, i], (gx, block_of(q ^ m, y))).start()

    def along_y(i):
        beta = i ^ across
        drain(w.at[beta, y], w_recv.at[0, i])
        for piece in range(4):
            mine = w.at[beta, y, piece]
            for m in (1, 3, 2):
                remote(mine, mine, pass_sent, w_recv.at[1, i], (gx, block_of(q, y ^ m))).start()

    def send_v():
        for m in range(8):
            gx2 = gx ^ m
            z2 = gx2 >> 2
            for e in range(2):
                q2 = z2 if e == 0 else 3 - z2
                src, dst = own_v.at[q2 * 4 + (gx2 & 3)], v.at[gx, e]
                if m == 0:
                    pltpu.make_async_copy(src, dst, v_recv).start()
                else:
                    remote(src, dst, v_sent, v_recv, (gx2, gy)).start()

    first = lax.broadcasted_iota(jnp.int32, (32, 128), 1) < 64

    def low(part, beta):
        for g in range(16):
            gq, g_y = ((g >> 3) << 1) | (g & 1), (g >> 1) & 3
            rows = x[part, :, g, beta].reshape(64, 128)
            table = w[beta, g_y, gq, 0:2].reshape(64, 128)
            got = lax.dot_general(
                table, rows, (((1,), (1,)), ((), ())), preferred_element_type=F32)
            pair = jnp.concatenate([got[:32], got[32:]], axis=1)
            low_state[0, g] = pair.astype(BF16)
            low_turned[0, g] = turn(pair, first)
        for level in range(4):
            now, later = level % 2, (level + 1) % 2
            for g in range(16):
                h = g ^ (1 << level)
                if h < g:
                    continue
                right = jnp.concatenate(
                    [low_state[now, g], low_state[now, h],
                     low_turned[now, g], low_turned[now, h]], axis=0)
                left = jnp.concatenate(
                    [w[beta, (i >> 1) & 3, ((i >> 3) << 1) | (i & 1), 2 + level] for i in (g, h)],
                    axis=0)
                both = jnp.dot(left, right, preferred_element_type=F32)
                for box, got in ((g, both[:32]), (h, both[32:])):
                    if level == 3:
                        o[part, beta, box] = got.astype(BF16)
                    else:
                        low_state[later, box] = got.astype(BF16)
                        low_turned[later, box] = turn(got, first)

    def send_o(part):
        spread = (across << 1) ^ (zl << 3)

        def each(i, carry):
            beta = (i & 3) ^ across
            gx2 = z_of(q) * 4 + beta
            gy2 = gy ^ (i >> 2) ^ ((i & 3) << 1) ^ spread
            src, dst = o.at[part, beta, gy2], t.at[part, gx, q >> 1, y]
            mine = (gx2 == gx) & (gy2 == gy)

            @pl.when(mine)
            def _():
                pltpu.make_async_copy(src, dst, t_recv.at[part]).start()

            @pl.when(jnp.logical_not(mine))
            def _():
                remote(src, dst, o_sent, t_recv.at[part], (gx2, gy2)).start()
            return carry

        lax.fori_loop(0, 64, each, 0)

    def high(part):
        def box_of(e, carry):
            for g in range(8):
                for side in range(4):
                    lanes = slice(side * 128, side * 128 + 128)
                    tile = t[part, g, e, side]
                    high_state[0, g, :, lanes] = tile
                    high_turned[0, g, :, lanes] = turn(tile.astype(F32), first)
            for level in range(3):
                now, later = level % 2, (level + 1) % 2
                for g in range(8):
                    h = g ^ (1 << level)
                    if h < g:
                        continue
                    right = jnp.concatenate(
                        [high_state[now, g], high_state[now, h],
                         high_turned[now, g], high_turned[now, h]], axis=0)
                    left = jnp.concatenate([v[g, e, level], v[h, e, level]], axis=0)
                    both = jnp.dot(left, right, preferred_element_type=F32)
                    for box, got in ((g, both[:32]), (h, both[32:])):
                        piece = [got[:, i * 128:i * 128 + 128] for i in range(4)]
                        if level == 2:
                            for two in range(2):
                                one, other = piece[2 * two], piece[2 * two + 1]
                                f[part, box, e, two, 0] = jnp.where(
                                    first, one, pltpu.roll(other, 64, 1)).astype(BF16)
                                f[part, box, e, two, 1] = jnp.where(
                                    first, pltpu.roll(one, 64, 1), other).astype(BF16)
                        else:
                            high_state[later, box] = got.astype(BF16)
                            for i in range(4):
                                high_turned[later, box, :, i * 128:i * 128 + 128] = turn(
                                    piece[i], first)
            return carry

        lax.fori_loop(0, 2, box_of, 0)

    def send_f(part):
        for m in range(1, 8):
            remote(f.at[part, gx ^ m], g_ref.at[gx, part], f_sent, g_recv, (gx ^ m, gy)).start()
        pltpu.make_async_copy(f.at[part, gx], g_ref.at[gx, part], g_recv).start()

    def low_part(part, weights):
        def each(i, carry):
            if weights:
                drain(w.at[pl.ds(0, 3), 0], w_recv.at[1, i])
            low(part, i ^ across)
            return carry

        drain(x.at[part], x_recv.at[part])
        lax.fori_loop(0, 4, each, 0)
        send_o(part)

    def high_part(part):
        drain(t.at[part], t_recv.at[part])
        high(part)
        send_f(part)

    own(0)
    own(1)
    own(2)
    own(3)
    send_samples(0, (0, 1, 2, 3))
    send_samples(1, (0, 1, 2, 3))
    along_y(0)
    send_samples(0, (4,))
    send_samples(2, (5,))
    send_samples(2, (2,))
    send_samples(0, (5,))
    send_samples(2, (4,))
    send_samples(2, (3,))
    along_y(1)
    send_samples(0, (6,))
    send_samples(2, (7,))
    send_samples(2, (0,))
    send_samples(0, (7,))
    send_samples(2, (6,))
    send_samples(2, (1,))
    along_y(2)
    send_samples(1, (4,))
    send_samples(3, (5,))
    send_samples(3, (2,))
    send_samples(1, (5,))
    send_samples(3, (4,))
    send_samples(3, (3,))
    along_y(3)
    send_samples(1, (6,))
    send_samples(3, (7,))
    send_samples(3, (0,))
    send_samples(1, (7,))
    send_samples(3, (6,))
    send_samples(3, (1,))
    send_v()
    for step in range(PARTS + 2):
        if step < PARTS:
            low_part(((0, 2, 1, 3))[step], step == 0)
        if step == 2:
            drain(v, v_recv)
        if step >= 2:
            high_part(((0, 2, 1, 3))[step - 2])
    drain(g_ref, g_recv)
    drain(f.at[:, pl.ds(0, 7)], f_sent)
    drain(x.at[pl.ds(0, 3)], x_sent)
    drain(x.at[3, pl.ds(0, 7)], x_sent)
    drain(own_w.at[pl.ds(0, 12)], w_sent)
    drain(w.at[pl.ds(0, 3)], pass_sent)
    drain(v.at[pl.ds(0, 7)], v_sent)
    drain(o.at[:, pl.ds(0, 3)], o_sent)

    @pl.when(own_z)
    def _():
        drain(o.at[:, 3, pl.ds(0, 15)], o_sent)

    @pl.when(jnp.logical_not(own_z))
    def _():
        drain(o.at[:, 3], o_sent)


def main(samples, interp, translation):
    dma = pltpu.SemaphoreType.DMA
    return pl.pallas_call(
        main_kernel,
        out_shape=jax.ShapeDtypeStruct((8, PARTS, 2, 2, 2, 32, 128), BF16),
        in_specs=[ANY] * 3,
        out_specs=ANY,
        scratch_shapes=[
            pltpu.VMEM((PARTS, 8, 16, 4, 8, 128), BF16),
            pltpu.VMEM((7, 2, 16, 32, 64), BF16),
            pltpu.VMEM((16, 6, 32, 128), BF16),
            pltpu.VMEM((16, 3, 32, 128), BF16),
            pltpu.VMEM((4, 4, 4, 6, 32, 128), BF16),
            pltpu.VMEM((8, 2, 3, 32, 128), BF16),
            pltpu.VMEM((PARTS, 4, 16, 32, 128), BF16),
            pltpu.VMEM((PARTS, 8, 2, 4, 32, 128), BF16),
            pltpu.VMEM((PARTS, 8, 2, 2, 2, 32, 128), BF16),
            pltpu.VMEM((2, 16, 32, 128), BF16),
            pltpu.VMEM((2, 16, 32, 128), BF16),
            pltpu.VMEM((2, 8, 32, 512), BF16),
            pltpu.VMEM((2, 8, 32, 512), BF16),
            dma((PARTS,)), dma((2, 4)), dma((PARTS,)), dma((8,)), dma((3,)),
        ],
        compiler_params=pltpu.CompilerParams(
            collective_id=1, has_side_effects=True, vmem_limit_bytes=LIMIT),
        cost_estimate=pl.CostEstimate(
            flops=2 * 2**30, bytes_accessed=10 * 2**20, transcendentals=0),
        name="levels",
    )(samples, interp, translation)


def turn(pair, first):
    moved = pltpu.roll(pair, 64, 1)
    return jnp.where(first, -moved, moved).astype(BF16)


def last_kernel(g_ref, e_ref, r_ref, g, r, load, store):
    places = [(z_of(k >> 1) * 4 + (k & 1) * 2, k >> 2) for k in range(8)]
    loads = [pltpu.make_async_copy(g_ref.at[pl.ds(a, 2), :, e], g.at[pl.ds(a, 2), :, e], load.at[k])
             for k, (a, e) in enumerate(places)]
    for copy in loads:
        copy.start()
    table = jnp.concatenate([e_ref[0], -e_ref[1]], axis=0)
    none = jnp.zeros((64, 128), BF16)
    stores = []
    for k, (a, e) in enumerate(places):
        at = k * 256
        pair = jnp.concatenate(
            [jnp.concatenate([table[:, at:at + 128], none], axis=1),
             jnp.concatenate([none, table[:, at + 128:at + 256]], axis=1)], axis=0)
        loads[k].wait()
        for part in range(PARTS):
            for two in range(2):
                left = jnp.concatenate(
                    [g[a + i, part, e, two].reshape(64, 128) for i in range(2)], axis=0)
                got = lax.dot_general(
                    left, pair, (((0,), (0,)), ((), ())), preferred_element_type=F32)
                got = got.reshape(2, 8, 8, 256)
                for side in range(2):
                    gy1 = block_of((k >> 1) ^ part, 2 * two + side)
                    r[:, gy1, :, at:at + 256] = got[side]
        if k % 2 == 1:
            wide = pl.ds(at - 256, 512)
            copy = pltpu.make_async_copy(
                r.at[:, :, :, wide], r_ref.at[:, :, :, wide], store.at[k // 2])
            copy.start()
            stores.append(copy)
    for copy in stores:
        copy.wait()


def last(g, e):
    dma = pltpu.SemaphoreType.DMA
    return pl.pallas_call(
        last_kernel,
        out_shape=jax.ShapeDtypeStruct((8, 16, 8, 2048), F32),
        in_specs=[ANY, pl.BlockSpec(memory_space=pltpu.VMEM)],
        out_specs=ANY,
        scratch_shapes=[pltpu.VMEM(g.shape, BF16), pltpu.VMEM((8, 16, 8, 2048), F32),
                        dma((8,)), dma((4,))],
        compiler_params=pltpu.CompilerParams(vmem_limit_bytes=LIMIT),
        name="last",
    )(g, e)


def on_device(samples, interp, translation, evaluate):
    by_box = samples.reshape(8, 2048, 128).transpose(1, 0, 2).reshape(8, 16, 16, 8, 128)
    state = main(by_box, interp, translation)
    return last(state, evaluate.transpose(0, 2, 1)).reshape(1024, 2048)


def solution(mesh):
    in_specs = (
        P(("gx", "gy"), None),
        P(None, ("gx", "gy"), None, None),
        P(None, None, ("gx", "gy"), None, None),
        P(None, ("gx", "gy"), None),
    )
    out_specs = P(None, ("gx", "gy"))
    return jax.shard_map(
        on_device, mesh=mesh, in_specs=in_specs, out_specs=out_specs, check_vma=False
    )
```

```python
import jax
import jax.numpy as jnp
from jax import lax
from jax.experimental import pallas as pl
from jax.experimental.pallas import tpu as pltpu
from jax.sharding import PartitionSpec as P

MESH = pl.DeviceIdType.MESH
F32, BF16 = jnp.float32, jnp.bfloat16
ANY = pl.BlockSpec(memory_space=pl.ANY)
LIMIT = 56 * 2**20


def place():
    return lax.axis_index("gx"), lax.axis_index("gy")


PARTS = 4


def block_of(q, y):
    return ((q >> 1) << 3) | (y << 1) | (q & 1)


def z_of(q):
    return (q >> 1) ^ (q & 1)


def q_of(z, e):
    return z if e == 0 else 3 - z


def mixed(a, b):
    order = []
    for j in range(4):
        order += [(a, 4 + j), (b, 4 + (j ^ 1)), (b, j ^ 2)]
    return order


X_ONLY = [(part, m) for part in (0, 1) for m in range(4)]


def remote(src, dst, send, recv, device):
    return pltpu.make_async_remote_copy(
        src_ref=src, dst_ref=dst, send_sem=send, recv_sem=recv,
        device_id=device, device_id_type=MESH)


def drain(ref, sem):
    pltpu.make_async_copy(ref, ref, sem).wait()


def main_kernel(samples, interp, translation, g_ref,
                x, raw, own_w, own_v, w, v, o, t, f, low_state, low_turned, high_state, high_turned,
                x_recv, w_recv, t_recv, sent, here):
    gx, gy = place()
    across, zl = gx & 3, gx >> 2
    y, q = (gy >> 1) & 3, ((gy >> 3) << 1) | (gy & 1)
    x_sent, w_sent, pass_sent, v_sent, o_sent, f_sent, v_recv, g_recv = [sent.at[i] for i in range(8)]
    own_z = z_of(q) == zl

    load = [pltpu.make_async_copy(translation, raw, here.at[0]),
            pltpu.make_async_copy(interp.at[0], own_w.at[:, 0], here.at[1]),
            pltpu.make_async_copy(interp.at[1], own_w.at[:, 1], here.at[2])]
    for copy in load:
        copy.start()

    barrier = pltpu.get_barrier_semaphore()

    def hello(device):
        pl.semaphore_signal(barrier, inc=1, device_id=device, device_id_type=MESH)

    def hello_samples(i, carry):
        hello((gx ^ (i & 7), block_of(q ^ (i >> 3), y)))
        return carry

    lax.fori_loop(1, 32, hello_samples, 0)
    for m in (1, 2, 3):
        hello((gx, block_of(q, y ^ m)))
    for e in range(2):
        source_q = q_of(zl, e)

        def hello_state(i, carry):
            gx1, gy1 = i & 7, block_of(source_q, i >> 3)

            @pl.when((gx1 != gx) | (gy1 != gy))
            def _():
                hello((gx1, gy1))
            return carry

        lax.fori_loop(0, 32, hello_state, 0)

    for copy in load:
        copy.wait()
    low_half = lax.broadcasted_iota(jnp.int32, (32, 128), 1) % 64 < 32

    def pack(b, carry):
        for level in range(7):
            pair = jnp.concatenate([raw[level, 0, b], raw[level, 1, b]], axis=1)
            bit = (gy >> level) & 1 if level < 4 else (gx >> (level - 4)) & 1
            wide = pair.astype(F32)
            other = jnp.where(low_half, pltpu.roll(wide, 96, 1), pltpu.roll(wide, 32, 1))
            pair = jnp.where(bit == 1, other, wide).astype(BF16)
            if level < 4:
                own_w[b, 2 + level] = pair
            else:
                own_v[b, level - 4] = pair
        return carry

    lax.fori_loop(0, 16, pack, 0)
    pl.semaphore_wait(barrier, 31 + 3 + 64 - jnp.where(own_z, 1, 0))

    def send_samples(part, m, rows):
        to = block_of(q ^ part, y)
        src = samples.at[gx ^ m, rows, pl.ds((q ^ part) * 4, 4)]
        dst = x.at[part, gx, rows]
        if m == 0 and part == 0:
            pltpu.make_async_copy(src, dst, x_recv.at[part]).start()
        else:
            remote(src, dst, x_sent, x_recv.at[part], (gx ^ m, to)).start()

    def burst(pieces, begin, end):
        def each(h, carry):
            for part, m in pieces:
                send_samples(part, m, pl.ds(h * 4, 4))
            return carry

        lax.fori_loop(begin, end, each, 0)

    def own(i):
        beta = i ^ across
        for m in range(4):
            src, dst = own_w.at[(q ^ m) * 4 + beta], w.at[beta, y, q]
            if m == 0:
                pltpu.make_async_copy(src, dst, w_recv.at[0, i]).start()
            else:
                remote(src, dst, w_sent, w_recv.at[0, i], (gx, block_of(q ^ m, y))).start()

    def along_y(i):
        beta = i ^ across
        drain(w.at[beta, y], w_recv.at[0, i])
        for piece in range(4):
            mine = w.at[beta, y, piece]
            for m in (1, 3, 2):
                remote(mine, mine, pass_sent, w_recv.at[1, i], (gx, block_of(q, y ^ m))).start()

    def send_v():
        for m in range(8):
            gx2 = gx ^ m
            z2 = gx2 >> 2
            for e in range(2):
                q2 = z2 if e == 0 else 3 - z2
                src, dst = own_v.at[q2 * 4 + (gx2 & 3)], v.at[gx, e]
                if m == 0:
                    pltpu.make_async_copy(src, dst, v_recv).start()
                else:
                    remote(src, dst, v_sent, v_recv, (gx2, gy)).start()

    first = lax.broadcasted_iota(jnp.int32, (32, 128), 1) < 64

    def low(part, beta):
        for g in range(16):
            gq, g_y = ((g >> 3) << 1) | (g & 1), (g >> 1) & 3
            rows = x[part, :, g, beta].reshape(64, 128)
            table = w[beta, g_y, gq, 0:2].reshape(64, 128)
            got = lax.dot_general(
                table, rows, (((1,), (1,)), ((), ())), preferred_element_type=F32)
            pair = jnp.concatenate([got[:32], got[32:]], axis=1)
            low_state[0, g] = pair.astype(BF16)
            low_turned[0, g] = turn(pair, first)
        for level in range(4):
            now, later = level % 2, (level + 1) % 2
            for g in range(16):
                h = g ^ (1 << level)
                if h < g:
                    continue
                right = jnp.concatenate(
                    [low_state[now, g], low_state[now, h],
                     low_turned[now, g], low_turned[now, h]], axis=0)
                left = jnp.concatenate(
                    [w[beta, (i >> 1) & 3, ((i >> 3) << 1) | (i & 1), 2 + level] for i in (g, h)],
                    axis=0)
                both = jnp.dot(left, right, preferred_element_type=F32)
                for box, got in ((g, both[:32]), (h, both[32:])):
                    if level == 3:
                        o[part, beta, box] = got.astype(BF16)
                    else:
                        low_state[later, box] = got.astype(BF16)
                        low_turned[later, box] = turn(got, first)

    def send_o(part):
        spread = (across << 1) ^ (zl << 3)

        def each(i, carry):
            beta = (i & 3) ^ across
            gx2 = z_of(q) * 4 + beta
            gy2 = gy ^ (i >> 2) ^ ((i & 3) << 1) ^ spread
            src, dst = o.at[part, beta, gy2], t.at[part, gx, q >> 1, y]
            mine = (gx2 == gx) & (gy2 == gy)

            @pl.when(mine)
            def _():
                pltpu.make_async_copy(src, dst, t_recv.at[part]).start()

            @pl.when(jnp.logical_not(mine))
            def _():
                remote(src, dst, o_sent, t_recv.at[part], (gx2, gy2)).start()
            return carry

        lax.fori_loop(0, 64, each, 0)

    def high(part):
        def box_of(e, carry):
            for g in range(8):
                for side in range(4):
                    lanes = slice(side * 128, side * 128 + 128)
                    tile = t[part, g, e, side]
                    high_state[0, g, :, lanes] = tile
                    high_turned[0, g, :, lanes] = turn(tile.astype(F32), first)
            for level in range(3):
                now, later = level % 2, (level + 1) % 2
                for g in range(8):
                    h = g ^ (1 << level)
                    if h < g:
                        continue
                    right = jnp.concatenate(
                        [high_state[now, g], high_state[now, h],
                         high_turned[now, g], high_turned[now, h]], axis=0)
                    left = jnp.concatenate([v[g, e, level], v[h, e, level]], axis=0)
                    both = jnp.dot(left, right, preferred_element_type=F32)
                    for box, got in ((g, both[:32]), (h, both[32:])):
                        piece = [got[:, i * 128:i * 128 + 128] for i in range(4)]
                        if level == 2:
                            for two in range(2):
                                one, other = piece[2 * two], piece[2 * two + 1]
                                f[part, box, e, two, 0] = jnp.where(
                                    first, one, pltpu.roll(other, 64, 1)).astype(BF16)
                                f[part, box, e, two, 1] = jnp.where(
                                    first, pltpu.roll(one, 64, 1), other).astype(BF16)
                        else:
                            high_state[later, box] = got.astype(BF16)
                            for i in range(4):
                                high_turned[later, box, :, i * 128:i * 128 + 128] = turn(
                                    piece[i], first)
            return carry

        lax.fori_loop(0, 2, box_of, 0)

    def send_f(part):
        for m in range(1, 8):
            remote(f.at[part, gx ^ m], g_ref.at[gx, part], f_sent, g_recv, (gx ^ m, gy)).start()
        pltpu.make_async_copy(f.at[part, gx], g_ref.at[gx, part], g_recv).start()

    def low_part(part, weights):
        def each(i, carry):
            if weights:
                drain(w.at[pl.ds(0, 3), 0], w_recv.at[1, i])
            low(part, i ^ across)
            return carry

        drain(x.at[part], x_recv.at[part])
        lax.fori_loop(0, 4, each, 0)
        send_o(part)

    def high_part(part):
        drain(t.at[part], t_recv.at[part])
        high(part)
        send_f(part)

    own(0)
    own(1)
    own(2)
    own(3)
    burst(X_ONLY, 0, 4)
    along_y(0)
    burst(mixed(0, 2), 0, 2)
    along_y(1)
    burst(mixed(0, 2), 2, 4)
    along_y(2)
    burst(mixed(1, 3), 0, 2)
    along_y(3)
    burst(mixed(1, 3), 2, 4)
    send_v()
    for step in range(PARTS + 2):
        if step < PARTS:
            low_part(((0, 2, 1, 3))[step], step == 0)
        if step == 2:
            drain(v, v_recv)
        if step >= 2:
            high_part(((0, 2, 1, 3))[step - 2])
    drain(g_ref, g_recv)
    drain(f.at[:, pl.ds(0, 7)], f_sent)
    drain(x.at[pl.ds(0, 3)], x_sent)
    drain(x.at[3, pl.ds(0, 7)], x_sent)
    drain(own_w.at[pl.ds(0, 12)], w_sent)
    drain(w.at[pl.ds(0, 3)], pass_sent)
    drain(v.at[pl.ds(0, 7)], v_sent)
    drain(o.at[:, pl.ds(0, 3)], o_sent)

    @pl.when(own_z)
    def _():
        drain(o.at[:, 3, pl.ds(0, 15)], o_sent)

    @pl.when(jnp.logical_not(own_z))
    def _():
        drain(o.at[:, 3], o_sent)


def main(samples, interp, translation):
    dma = pltpu.SemaphoreType.DMA
    return pl.pallas_call(
        main_kernel,
        out_shape=jax.ShapeDtypeStruct((8, PARTS, 2, 2, 2, 32, 128), BF16),
        in_specs=[ANY] * 3,
        out_specs=ANY,
        scratch_shapes=[
            pltpu.VMEM((PARTS, 8, 16, 4, 8, 128), BF16),
            pltpu.VMEM((7, 2, 16, 32, 64), BF16),
            pltpu.VMEM((16, 6, 32, 128), BF16),
            pltpu.VMEM((16, 3, 32, 128), BF16),
            pltpu.VMEM((4, 4, 4, 6, 32, 128), BF16),
            pltpu.VMEM((8, 2, 3, 32, 128), BF16),
            pltpu.VMEM((PARTS, 4, 16, 32, 128), BF16),
            pltpu.VMEM((PARTS, 8, 2, 4, 32, 128), BF16),
            pltpu.VMEM((PARTS, 8, 2, 2, 2, 32, 128), BF16),
            pltpu.VMEM((2, 16, 32, 128), BF16),
            pltpu.VMEM((2, 16, 32, 128), BF16),
            pltpu.VMEM((2, 8, 32, 512), BF16),
            pltpu.VMEM((2, 8, 32, 512), BF16),
            dma((PARTS,)), dma((2, 4)), dma((PARTS,)), dma((8,)), dma((3,)),
        ],
        compiler_params=pltpu.CompilerParams(
            collective_id=1, has_side_effects=True, vmem_limit_bytes=LIMIT),
        cost_estimate=pl.CostEstimate(
            flops=2 * 2**30, bytes_accessed=10 * 2**20, transcendentals=0),
        name="levels",
    )(samples, interp, translation)


def turn(pair, first):
    moved = pltpu.roll(pair, 64, 1)
    return jnp.where(first, -moved, moved).astype(BF16)


def last_kernel(g_ref, e_ref, r_ref, g, r, load, store):
    places = [(z_of(k >> 1) * 4 + (k & 1) * 2, k >> 2) for k in range(8)]
    loads = [pltpu.make_async_copy(g_ref.at[pl.ds(a, 2), :, e], g.at[pl.ds(a, 2), :, e], load.at[k])
             for k, (a, e) in enumerate(places)]
    for copy in loads:
        copy.start()
    table = jnp.concatenate([e_ref[0], -e_ref[1]], axis=0)
    none = jnp.zeros((64, 128), BF16)
    stores = []
    for k, (a, e) in enumerate(places):
        at = k * 256
        pair = jnp.concatenate(
            [jnp.concatenate([table[:, at:at + 128], none], axis=1),
             jnp.concatenate([none, table[:, at + 128:at + 256]], axis=1)], axis=0)
        loads[k].wait()
        for part in range(PARTS):
            for two in range(2):
                left = jnp.concatenate(
                    [g[a + i, part, e, two].reshape(64, 128) for i in range(2)], axis=0)
                got = lax.dot_general(
                    left, pair, (((0,), (0,)), ((), ())), preferred_element_type=F32)
                got = got.reshape(2, 8, 8, 256)
                for side in range(2):
                    gy1 = block_of((k >> 1) ^ part, 2 * two + side)
                    r[:, gy1, :, at:at + 256] = got[side]
        if k % 2 == 1:
            wide = pl.ds(at - 256, 512)
            copy = pltpu.make_async_copy(
                r.at[:, :, :, wide], r_ref.at[:, :, :, wide], store.at[k // 2])
            copy.start()
            stores.append(copy)
    for copy in stores:
        copy.wait()


def last(g, e):
    dma = pltpu.SemaphoreType.DMA
    return pl.pallas_call(
        last_kernel,
        out_shape=jax.ShapeDtypeStruct((8, 16, 8, 2048), F32),
        in_specs=[ANY, pl.BlockSpec(memory_space=pltpu.VMEM)],
        out_specs=ANY,
        scratch_shapes=[pltpu.VMEM(g.shape, BF16), pltpu.VMEM((8, 16, 8, 2048), F32),
                        dma((8,)), dma((4,))],
        compiler_params=pltpu.CompilerParams(vmem_limit_bytes=LIMIT),
        name="last",
    )(g, e)


def on_device(samples, interp, translation, evaluate):
    by_box = samples.reshape(8, 2048, 128).transpose(1, 0, 2).reshape(8, 16, 16, 8, 128)
    state = main(by_box, interp, translation)
    return last(state, evaluate.transpose(0, 2, 1)).reshape(1024, 2048)


def solution(mesh):
    in_specs = (
        P(("gx", "gy"), None),
        P(None, ("gx", "gy"), None, None),
        P(None, None, ("gx", "gy"), None, None),
        P(None, ("gx", "gy"), None),
    )
    out_specs = P(None, ("gx", "gy"))
    return jax.shard_map(
        on_device, mesh=mesh, in_specs=in_specs, out_specs=out_specs, check_vma=False
    )
```

```python
import jax
import jax.numpy as jnp
from jax import lax
from jax.experimental import pallas as pl
from jax.experimental.pallas import tpu as pltpu
from jax.sharding import PartitionSpec as P

MESH = pl.DeviceIdType.MESH
F32, BF16 = jnp.float32, jnp.bfloat16
ANY = pl.BlockSpec(memory_space=pl.ANY)
LIMIT = 56 * 2**20


def place():
    return lax.axis_index("gx"), lax.axis_index("gy")


PARTS = 4


def block_of(q, y):
    return ((q >> 1) << 3) | (y << 1) | (q & 1)


def z_of(q):
    return (q >> 1) ^ (q & 1)


def q_of(z, e):
    return z if e == 0 else 3 - z


def mixed(a, b):
    order = []
    for j in range(4):
        order += [(a, 4 + j), (b, 4 + (j ^ 1)), (b, j ^ 2)]
    return order


X_ONLY = [(part, m) for part in (0, 1) for m in range(4)]


def remote(src, dst, send, recv, device):
    return pltpu.make_async_remote_copy(
        src_ref=src, dst_ref=dst, send_sem=send, recv_sem=recv,
        device_id=device, device_id_type=MESH)


def drain(ref, sem):
    pltpu.make_async_copy(ref, ref, sem).wait()


def main_kernel(samples, interp, translation, g_ref,
                x, raw, own_w, own_v, w, v, o, t, f, low_state, low_turned, high_state, high_turned,
                x_recv, w_recv, t_recv, sent, here):
    gx, gy = place()
    across, zl = gx & 3, gx >> 2
    y, q = (gy >> 1) & 3, ((gy >> 3) << 1) | (gy & 1)
    x_sent, w_sent, pass_sent, v_sent, o_sent, f_sent, v_recv, g_recv = [sent.at[i] for i in range(8)]
    own_z = z_of(q) == zl

    load = [pltpu.make_async_copy(translation, raw, here.at[0]),
            pltpu.make_async_copy(interp.at[0], own_w.at[:, 0], here.at[1]),
            pltpu.make_async_copy(interp.at[1], own_w.at[:, 1], here.at[2])]
    for copy in load:
        copy.start()

    barrier = pltpu.get_barrier_semaphore()

    def hello(device):
        pl.semaphore_signal(barrier, inc=1, device_id=device, device_id_type=MESH)

    def hello_samples(i, carry):
        hello((gx ^ (i & 7), block_of(q ^ (i >> 3), y)))
        return carry

    lax.fori_loop(1, 32, hello_samples, 0)
    for m in (1, 2, 3):
        hello((gx, block_of(q, y ^ m)))
    for e in range(2):
        source_q = q_of(zl, e)

        def hello_state(i, carry):
            gx1, gy1 = i & 7, block_of(source_q, i >> 3)

            @pl.when((gx1 != gx) | (gy1 != gy))
            def _():
                hello((gx1, gy1))
            return carry

        lax.fori_loop(0, 32, hello_state, 0)

    for copy in load:
        copy.wait()
    low_half = lax.broadcasted_iota(jnp.int32, (32, 128), 1) % 64 < 32

    def pack(b, carry):
        for level in range(7):
            pair = jnp.concatenate([raw[level, 0, b], raw[level, 1, b]], axis=1)
            bit = (gy >> level) & 1 if level < 4 else (gx >> (level - 4)) & 1
            wide = pair.astype(F32)
            other = jnp.where(low_half, pltpu.roll(wide, 96, 1), pltpu.roll(wide, 32, 1))
            pair = jnp.where(bit == 1, other, wide).astype(BF16)
            if level < 4:
                own_w[b, 2 + level] = pair
            else:
                own_v[b, level - 4] = pair
        return carry

    lax.fori_loop(0, 16, pack, 0)
    pl.semaphore_wait(barrier, 31 + 3 + 64 - jnp.where(own_z, 1, 0))

    def send_samples(part, m, rows):
        to = block_of(q ^ part, y)
        src = samples.at[gx ^ m, rows, pl.ds((q ^ part) * 4, 4)]
        dst = x.at[part, gx, rows]
        if m == 0 and part == 0:
            pltpu.make_async_copy(src, dst, x_recv.at[part]).start()
        else:
            remote(src, dst, x_sent, x_recv.at[part], (gx ^ m, to)).start()

    def burst(pieces, begin, end):
        def each(h, carry):
            for part, m in pieces:
                send_samples(part, m, pl.ds(h * 4, 4))
            return carry

        lax.fori_loop(begin, end, each, 0)

    def own(i):
        beta = i ^ across
        for m in range(4):
            src, dst = own_w.at[(q ^ m) * 4 + beta], w.at[beta, y, q]
            if m == 0:
                pltpu.make_async_copy(src, dst, w_recv.at[0, i]).start()
            else:
                remote(src, dst, w_sent, w_recv.at[0, i], (gx, block_of(q ^ m, y))).start()

    def along_y(i):
        beta = i ^ across
        drain(w.at[beta, y], w_recv.at[0, i])
        for piece in range(4):
            mine = w.at[beta, y, piece]
            for m in (1, 3, 2):
                remote(mine, mine, pass_sent, w_recv.at[1, i], (gx, block_of(q, y ^ m))).start()

    def send_v():
        for m in range(8):
            gx2 = gx ^ m
            z2 = gx2 >> 2
            for e in range(2):
                q2 = z2 if e == 0 else 3 - z2
                src, dst = own_v.at[q2 * 4 + (gx2 & 3)], v.at[gx, e]
                if m == 0:
                    pltpu.make_async_copy(src, dst, v_recv).start()
                else:
                    remote(src, dst, v_sent, v_recv, (gx2, gy)).start()

    first = lax.broadcasted_iota(jnp.int32, (32, 128), 1) < 64

    def low(part, beta):
        for g in range(16):
            gq, g_y = ((g >> 3) << 1) | (g & 1), (g >> 1) & 3
            rows = x[part, :, g, beta].reshape(64, 128)
            table = w[beta, g_y, gq, 0:2].reshape(64, 128)
            got = lax.dot_general(
                table, rows, (((1,), (1,)), ((), ())), preferred_element_type=F32)
            pair = jnp.concatenate([got[:32], got[32:]], axis=1)
            low_state[0, g] = pair.astype(BF16)
            low_turned[0, g] = turn(pair, first)
        for level in range(4):
            now, later = level % 2, (level + 1) % 2
            for g in range(16):
                h = g ^ (1 << level)
                if h < g:
                    continue
                right = jnp.concatenate(
                    [low_state[now, g], low_state[now, h],
                     low_turned[now, g], low_turned[now, h]], axis=0)
                left = jnp.concatenate(
                    [w[beta, (i >> 1) & 3, ((i >> 3) << 1) | (i & 1), 2 + level] for i in (g, h)],
                    axis=0)
                both = jnp.dot(left, right, preferred_element_type=F32)
                for box, got in ((g, both[:32]), (h, both[32:])):
                    if level == 3:
                        o[part, beta, box] = got.astype(BF16)
                    else:
                        low_state[later, box] = got.astype(BF16)
                        low_turned[later, box] = turn(got, first)

    def send_o(part):
        spread = (across << 1) ^ (zl << 3)

        def each(i, carry):
            beta = (i & 3) ^ across
            gx2 = z_of(q) * 4 + beta
            gy2 = gy ^ (i >> 2) ^ ((i & 3) << 1) ^ spread
            src, dst = o.at[part, beta, gy2], t.at[part, gx, q >> 1, y]
            mine = (gx2 == gx) & (gy2 == gy)

            @pl.when(mine)
            def _():
                pltpu.make_async_copy(src, dst, t_recv.at[part]).start()

            @pl.when(jnp.logical_not(mine))
            def _():
                remote(src, dst, o_sent, t_recv.at[part], (gx2, gy2)).start()
            return carry

        lax.fori_loop(0, 64, each, 0)

    def high(part):
        def box_of(e, carry):
            for g in range(8):
                for side in range(4):
                    lanes = slice(side * 128, side * 128 + 128)
                    tile = t[part, g, e, side]
                    high_state[0, g, :, lanes] = tile
                    high_turned[0, g, :, lanes] = turn(tile.astype(F32), first)
            for level in range(3):
                now, later = level % 2, (level + 1) % 2
                for g in range(8):
                    h = g ^ (1 << level)
                    if h < g:
                        continue
                    right = jnp.concatenate(
                        [high_state[now, g], high_state[now, h],
                         high_turned[now, g], high_turned[now, h]], axis=0)
                    left = jnp.concatenate([v[g, e, level], v[h, e, level]], axis=0)
                    both = jnp.dot(left, right, preferred_element_type=F32)
                    for box, got in ((g, both[:32]), (h, both[32:])):
                        piece = [got[:, i * 128:i * 128 + 128] for i in range(4)]
                        if level == 2:
                            for two in range(2):
                                one, other = piece[2 * two], piece[2 * two + 1]
                                f[part, box, e, two, 0] = jnp.where(
                                    first, one, pltpu.roll(other, 64, 1)).astype(BF16)
                                f[part, box, e, two, 1] = jnp.where(
                                    first, pltpu.roll(one, 64, 1), other).astype(BF16)
                        else:
                            high_state[later, box] = got.astype(BF16)
                            for i in range(4):
                                high_turned[later, box, :, i * 128:i * 128 + 128] = turn(
                                    piece[i], first)
            return carry

        lax.fori_loop(0, 2, box_of, 0)

    def send_f(part):
        for m in range(1, 8):
            remote(f.at[part, gx ^ m], g_ref.at[gx, part], f_sent, g_recv, (gx ^ m, gy)).start()
        pltpu.make_async_copy(f.at[part, gx], g_ref.at[gx, part], g_recv).start()

    def low_part(part, weights):
        def each(i, carry):
            if weights:
                drain(w.at[pl.ds(0, 3), 0], w_recv.at[1, i])
            low(part, i ^ across)
            return carry

        drain(x.at[part], x_recv.at[part])
        lax.fori_loop(0, 4, each, 0)
        send_o(part)

    def high_part(part):
        drain(t.at[part], t_recv.at[part])
        high(part)
        send_f(part)

    own(0)
    own(1)
    own(2)
    own(3)
    burst(X_ONLY, 0, 4)
    along_y(0)
    along_y(1)
    burst(mixed(0, 2), 0, 4)
    along_y(2)
    burst(mixed(1, 3), 0, 2)
    along_y(3)
    burst(mixed(1, 3), 2, 4)
    send_v()
    for step in range(PARTS + 2):
        if step < PARTS:
            low_part(((0, 2, 1, 3))[step], step == 0)
        if step == 2:
            drain(v, v_recv)
        if step >= 2:
            high_part(((0, 2, 1, 3))[step - 2])
    drain(g_ref, g_recv)
    drain(f.at[:, pl.ds(0, 7)], f_sent)
    drain(x.at[pl.ds(0, 3)], x_sent)
    drain(x.at[3, pl.ds(0, 7)], x_sent)
    drain(own_w.at[pl.ds(0, 12)], w_sent)
    drain(w.at[pl.ds(0, 3)], pass_sent)
    drain(v.at[pl.ds(0, 7)], v_sent)
    drain(o.at[:, pl.ds(0, 3)], o_sent)

    @pl.when(own_z)
    def _():
        drain(o.at[:, 3, pl.ds(0, 15)], o_sent)

    @pl.when(jnp.logical_not(own_z))
    def _():
        drain(o.at[:, 3], o_sent)


def main(samples, interp, translation):
    dma = pltpu.SemaphoreType.DMA
    return pl.pallas_call(
        main_kernel,
        out_shape=jax.ShapeDtypeStruct((8, PARTS, 2, 2, 2, 32, 128), BF16),
        in_specs=[ANY] * 3,
        out_specs=ANY,
        scratch_shapes=[
            pltpu.VMEM((PARTS, 8, 16, 4, 8, 128), BF16),
            pltpu.VMEM((7, 2, 16, 32, 64), BF16),
            pltpu.VMEM((16, 6, 32, 128), BF16),
            pltpu.VMEM((16, 3, 32, 128), BF16),
            pltpu.VMEM((4, 4, 4, 6, 32, 128), BF16),
            pltpu.VMEM((8, 2, 3, 32, 128), BF16),
            pltpu.VMEM((PARTS, 4, 16, 32, 128), BF16),
            pltpu.VMEM((PARTS, 8, 2, 4, 32, 128), BF16),
            pltpu.VMEM((PARTS, 8, 2, 2, 2, 32, 128), BF16),
            pltpu.VMEM((2, 16, 32, 128), BF16),
            pltpu.VMEM((2, 16, 32, 128), BF16),
            pltpu.VMEM((2, 8, 32, 512), BF16),
            pltpu.VMEM((2, 8, 32, 512), BF16),
            dma((PARTS,)), dma((2, 4)), dma((PARTS,)), dma((8,)), dma((3,)),
        ],
        compiler_params=pltpu.CompilerParams(
            collective_id=1, has_side_effects=True, vmem_limit_bytes=LIMIT),
        cost_estimate=pl.CostEstimate(
            flops=2 * 2**30, bytes_accessed=10 * 2**20, transcendentals=0),
        name="levels",
    )(samples, interp, translation)


def turn(pair, first):
    moved = pltpu.roll(pair, 64, 1)
    return jnp.where(first, -moved, moved).astype(BF16)


def last_kernel(g_ref, e_ref, r_ref, g, r, load, store):
    places = [(z_of(k >> 1) * 4 + (k & 1) * 2, k >> 2) for k in range(8)]
    loads = [pltpu.make_async_copy(g_ref.at[pl.ds(a, 2), :, e], g.at[pl.ds(a, 2), :, e], load.at[k])
             for k, (a, e) in enumerate(places)]
    for copy in loads:
        copy.start()
    table = jnp.concatenate([e_ref[0], -e_ref[1]], axis=0)
    none = jnp.zeros((64, 128), BF16)
    stores = []
    for k, (a, e) in enumerate(places):
        at = k * 256
        pair = jnp.concatenate(
            [jnp.concatenate([table[:, at:at + 128], none], axis=1),
             jnp.concatenate([none, table[:, at + 128:at + 256]], axis=1)], axis=0)
        loads[k].wait()
        for part in range(PARTS):
            for two in range(2):
                left = jnp.concatenate(
                    [g[a + i, part, e, two].reshape(64, 128) for i in range(2)], axis=0)
                got = lax.dot_general(
                    left, pair, (((0,), (0,)), ((), ())), preferred_element_type=F32)
                got = got.reshape(2, 8, 8, 256)
                for side in range(2):
                    gy1 = block_of((k >> 1) ^ part, 2 * two + side)
                    r[:, gy1, :, at:at + 256] = got[side]
        if k % 2 == 1 or k == 6:
            wide = pl.ds(at, 256) if k >= 6 else pl.ds(at - 256, 512)
            copy = pltpu.make_async_copy(
                r.at[:, :, :, wide], r_ref.at[:, :, :, wide], store.at[len(stores)])
            copy.start()
            stores.append(copy)
    for copy in stores:
        copy.wait()


def last(g, e):
    dma = pltpu.SemaphoreType.DMA
    return pl.pallas_call(
        last_kernel,
        out_shape=jax.ShapeDtypeStruct((8, 16, 8, 2048), F32),
        in_specs=[ANY, pl.BlockSpec(memory_space=pltpu.VMEM)],
        out_specs=ANY,
        scratch_shapes=[pltpu.VMEM(g.shape, BF16), pltpu.VMEM((8, 16, 8, 2048), F32),
                        dma((8,)), dma((5,))],
        compiler_params=pltpu.CompilerParams(vmem_limit_bytes=LIMIT),
        name="last",
    )(g, e)


def on_device(samples, interp, translation, evaluate):
    by_box = samples.reshape(8, 2048, 128).transpose(1, 0, 2).reshape(8, 16, 16, 8, 128)
    state = main(by_box, interp, translation)
    return last(state, evaluate.transpose(0, 2, 1)).reshape(1024, 2048)


def solution(mesh):
    in_specs = (
        P(("gx", "gy"), None),
        P(None, ("gx", "gy"), None, None),
        P(None, None, ("gx", "gy"), None, None),
        P(None, ("gx", "gy"), None),
    )
    out_specs = P(None, ("gx", "gy"))
    return jax.shard_map(
        on_device, mesh=mesh, in_specs=in_specs, out_specs=out_specs, check_vma=False
    )
```
